512 devices in a mesh: chan: 16 (over x, y), win: 32 (over z, core).
Axes of the slice: x: 4, y: 4, z: 16, core: 2. Of those that a mesh axis runs over, the one named last changes fastest.
Arguments:
- traces: float32 [1024, 64, 1024], P('chan', 'win'), may hold values from -80 to 80, as said below
- needed: int32 [16, 48], replicated, may hold values from 0 to 1023, as said below
- home_slot: int32 [32, 8], P('chan'), may hold values from 0 to 47, as said below
- partner_slot: int32 [32, 16], P('chan'), may hold values from 0 to 47, as said below
- live_blocks: int32 [16], P('chan'), may hold values from 1 to 2, as said below
Outputs:
- correlations: float32 [4096, 1024], P(('chan', 'win'))
The draws below stay inside these ranges and needn't reach their ends.
Inputs may be any that keep to these rules, and one draw needn't show every extreme that they name: `traces`: samples are bounded by the range. `needed`: each row lists 48 distinct channels in increasing order; row d holds exactly 6 channels of its own group d * 64 .. (d + 1) * 64 - 1 and at most 6 of any other group of 64 channels. `home_slot`: within one block the 8 home positions and 16 partner positions are all distinct. `partner_slot`: within one block the 8 home positions and 16 partner positions are all distinct. `live_blocks`: some owner uses all 2 slots and another owner uses only one.
All inputs are finite; a program needn't handle non-finite values.
Results may differ from the reference program's by a relative error of at most 0.0041.
Values may be sent and summed in bfloat16 or wider, within the bound.
No kernel may reach another device: no remote copies, remote signals or barrier semaphores. Data moves between devices by JAX's collectives and lax.ppermute only.
A program may use at most 64 MiB of HBM per device.

```python
import math
import jax
import jax.numpy as jnp
from jax import lax

NFFT = 1024
C_DEV = 64
BLK_OWN = 2
HOMES = 8
PARTNERS = 16
NEED = 48
CAP = 6
CHANNELS = 1024
WINDOWS = 64
PAIRS = 4096
N_CHAN = 16


def draw_traces(key, part):
    draw_keys = jax.random.split(key, 5)
    full_shape = (CHANNELS, WINDOWS, NFFT)
    row_shape = (CHANNELS, WINDOWS, 1)
    noise_part = jnp.clip(jax.random.normal(draw_keys[0], full_shape, jnp.float32), -4.0, 4.0)
    gain_rows = jnp.exp(jax.random.uniform(draw_keys[1], row_shape, jnp.float32, math.log(0.5), math.log(5.0)))
    peak_bins = jax.random.randint(draw_keys[2], row_shape, 1, NFFT // 2)
    peak_phase = jax.random.uniform(draw_keys[3], row_shape, jnp.float32, -math.pi, math.pi)
    height = jax.random.uniform(draw_keys[4], row_shape, jnp.float32, 0.0, 3.0)
    sample_index = jnp.arange(NFFT, dtype=jnp.int32)
    peak_angle = (peak_bins * sample_index % NFFT).astype(jnp.float32) * (2.0 * math.pi / NFFT) + peak_phase
    return gain_rows * (noise_part + height * jnp.cos(peak_angle))


def draw_needed(key, part):
    tokens = N_CHAN * CAP
    token_group = jnp.arange(tokens, dtype=jnp.int32) // CAP
    token_rank = jnp.arange(tokens, dtype=jnp.int32) % CAP
    order_keys = jax.random.split(jax.random.fold_in(key, 11), N_CHAN)
    row_keys = jax.random.split(jax.random.fold_in(key, 12), N_CHAN)
    shuffles = jax.vmap(lambda row_key: jax.random.permutation(row_key, C_DEV))(row_keys)[:, :CAP].astype(jnp.int32)

    def one_owner(owner_key, owner_index):
        shuffled = jax.random.permutation(owner_key, tokens).astype(jnp.int32)
        priority = jnp.where(token_group == owner_index, shuffled - tokens, shuffled)
        chosen = jnp.argsort(priority, stable=True)[:NEED]
        chosen_group = token_group[chosen]
        channel = chosen_group * C_DEV + shuffles[chosen_group, token_rank[chosen]]
        return jnp.sort(channel)
    return jax.vmap(one_owner)(order_keys, jnp.arange(N_CHAN, dtype=jnp.int32)).astype(jnp.int32)


def block_slots(key):
    block_keys = jax.random.split(jax.random.fold_in(key, 21), N_CHAN * BLK_OWN)
    return jax.vmap(lambda block_key: jax.random.permutation(block_key, NEED)[:HOMES + PARTNERS])(block_keys).astype(jnp.int32)


def draw_home_slot(key, part):
    return block_slots(key)[:, :HOMES]


def draw_partner_slot(key, part):
    return block_slots(key)[:, HOMES:]


def draw_live_blocks(key, part):
    counts = jax.random.randint(jax.random.fold_in(key, 31), (N_CHAN,), 1, BLK_OWN + 1)
    fullest = jax.random.randint(jax.random.fold_in(key, 32), (), 0, N_CHAN)
    step_away = jax.random.randint(jax.random.fold_in(key, 33), (), 1, N_CHAN)
    sparsest = (fullest + step_away) % N_CHAN
    owner_index = jnp.arange(N_CHAN, dtype=jnp.int32)
    counts = jnp.where(owner_index == sparsest, 1, counts)
    return jnp.where(owner_index == fullest, BLK_OWN, counts).astype(jnp.int32)


def setup_inputs(seed: int = 0) -> dict:
    seeds = jax.random.split(jax.random.key(seed), 6)
    traces = draw_traces(jax.random.fold_in(seeds[5], 71), 0)
    needed = draw_needed(jax.random.fold_in(seeds[5], 71), 0)
    home_slot = draw_home_slot(jax.random.fold_in(seeds[5], 71), 0)
    partner_slot = draw_partner_slot(jax.random.fold_in(seeds[5], 71), 0)
    live_blocks = draw_live_blocks(jax.random.fold_in(seeds[5], 71), 0)
    return {"traces": traces, "needed": needed, "home_slot": home_slot, "partner_slot": partner_slot, "live_blocks": live_blocks}


band_reach = 64

def forward_table(samples):
    freq_bins = samples // 2
    sample_index = jnp.arange(samples, dtype=jnp.int32)[:, None]
    freq_index = jnp.arange(freq_bins, dtype=jnp.int32)[None, :]
    phase_angle = (sample_index * freq_index % samples).astype(jnp.float32) * (2.0 * math.pi / samples)
    return jnp.concatenate([jnp.cos(phase_angle), -jnp.sin(phase_angle)], axis=1)

def inverse_table(samples):
    freq_bins = samples // 2
    freq_index = jnp.arange(freq_bins, dtype=jnp.int32)[:, None]
    lag_shift = (jnp.arange(samples, dtype=jnp.int32) - samples // 2) % samples
    phase_angle = (freq_index * lag_shift[None, :] % samples).astype(jnp.float32) * (2.0 * math.pi / samples)
    weight = jnp.where(freq_index == 0, 1.0, 2.0).astype(jnp.float32)
    return jnp.concatenate([weight * jnp.cos(phase_angle), -weight * jnp.sin(phase_angle)], axis=0)

def band_table(freq_bins):
    bin_index = jnp.arange(freq_bins, dtype=jnp.int32)
    inside = (jnp.abs(bin_index[:, None] - bin_index[None, :]) <= band_reach).astype(jnp.float32)
    return inside / lax.optimization_barrier(jnp.sum(inside, axis=0, keepdims=True))

def whiten(trace_rows):
    samples = trace_rows.shape[-1]
    freq_bins = samples // 2
    spectrum = jnp.dot(trace_rows, forward_table(samples), precision=lax.Precision.HIGHEST)
    power_bins = spectrum[:, :freq_bins] ** 2 + spectrum[:, freq_bins:] ** 2
    smooth = jnp.dot(power_bins, band_table(freq_bins), precision=lax.Precision.HIGHEST)
    factor = 1.0 / jnp.sqrt(smooth + 1e-05)
    return (spectrum * jnp.concatenate([factor, factor], axis=1)).astype(jnp.bfloat16)

def cross_spectra(home_spectra, partners):
    freq_bins = home_spectra.shape[-1] // 2
    home_f = home_spectra.astype(jnp.float32)
    part_f = partners.astype(jnp.float32)

    def product(left_side, right_side):
        return jnp.einsum('bhwf,bpwf->bhpf', left_side, right_side, precision=lax.Precision.HIGHEST)
    home_re, home_im = (home_f[..., :freq_bins], home_f[..., freq_bins:])
    part_re, part_im = (part_f[..., :freq_bins], part_f[..., freq_bins:])
    real_part = product(home_re, part_re) + product(home_im, part_im)
    imag_part = product(home_im, part_re) - product(home_re, part_im)
    joined = jnp.concatenate([real_part, imag_part], axis=-1)
    return joined.reshape(-1, joined.shape[-1])

def reference(traces, needed, home_slot, partner_slot, live_blocks):
    groups = traces.reshape(N_CHAN, C_DEV * WINDOWS, NFFT)
    whitened = lax.map(whiten, groups).reshape(CHANNELS, WINDOWS, NFFT)
    inverse = inverse_table(NFFT)
    norm_scale = 1.0 / math.sqrt(NFFT * WINDOWS)
    homes_all = home_slot.reshape(N_CHAN, BLK_OWN, HOMES)
    partners_all = partner_slot.reshape(N_CHAN, BLK_OWN, PARTNERS)
    block_index = jnp.arange(BLK_OWN * HOMES * PARTNERS, dtype=jnp.int32) // (HOMES * PARTNERS)

    def one_owner(packed):
        listed, home_rows, partner_rows, live_count = packed
        table_rows = whitened[listed]
        cross_terms = cross_spectra(table_rows[home_rows], table_rows[partner_rows])
        correlated = jnp.dot(cross_terms, inverse, precision=lax.Precision.HIGHEST) * norm_scale
        live_mask = (block_index < live_count).astype(jnp.float32)
        return correlated * live_mask[:, None]
    stacked = lax.map(one_owner, (needed, homes_all, partners_all, live_blocks))
    return stacked.reshape(PAIRS, NFFT)
```

```python
import math

import jax
import jax.numpy as jnp
import ml_dtypes
import numpy as np
from jax import lax
from jax.experimental import pallas as pl
from jax.experimental.pallas import tpu as pltpu
from jax.sharding import PartitionSpec as P

band_reach = 64
F32 = jnp.float32
BF16 = jnp.bfloat16


def halves(table):
    top = table.astype(ml_dtypes.bfloat16)
    rest = (table - top.astype(np.float64)).astype(ml_dtypes.bfloat16)
    return top, rest


def bin_order(freq_bins):
    return np.concatenate([np.arange(0, freq_bins, 2), np.arange(1, freq_bins, 2)])


def forward_tables(samples):
    n = np.arange(samples // 2)[:, None]
    parts = []
    for first in (0, 1):
        k = np.arange(first, samples // 2, 2)[None, :]
        angle = (n * k % samples) * (2.0 * math.pi / samples)
        parts.append(np.concatenate([np.cos(angle), -np.sin(angle)], axis=1))
    return halves(np.stack(parts))


def inverse_tables(samples):
    lag = np.arange(samples // 2)[None, :]
    parts = []
    for first in (0, 1):
        f = np.arange(first, samples // 2, 2)[:, None]
        angle = (f * lag % samples) * (2.0 * math.pi / samples)
        weight = np.where(f == 0, 1.0, 2.0)
        parts.append(np.concatenate([weight * np.cos(angle), -weight * np.sin(angle)], axis=0))
    return halves(np.stack(parts))


def band_tables(freq_bins):
    order = bin_order(freq_bins)
    inside = np.abs(order[:, None] - order[None, :]) <= band_reach
    share = 1.0 / inside.sum(axis=0, keepdims=True)
    return inside.astype(ml_dtypes.bfloat16), share.astype(np.float32)


def split(x):
    top = x.astype(BF16)
    return top, (x - top.astype(F32)).astype(BF16)


def dot(a, b):
    return jnp.dot(a, b, preferred_element_type=F32)


def product(x, table_top, table_rest):
    rows = x.shape[0]
    top, rest = split(x)
    both = dot(jnp.concatenate([top, rest], axis=0), table_top)
    return both[:rows] + both[rows:] + dot(top, table_rest)


def one_hot(index, size):
    spots = lax.broadcasted_iota(jnp.int32, (index.shape[0], size), 1)
    return jnp.where(spots == index, 1.0, 0.0).astype(BF16)


def spectra_kernel(x_ref, top_ref, rest_ref, band_ref, share_ref, index_ref, out_ref):
    half = x_ref.shape[1] // 2
    quarter = half // 2
    left, right = x_ref[:, :half], x_ref[:, half:]
    even = product(left + right, top_ref[0], rest_ref[0])
    odd = product(left - right, top_ref[1], rest_ref[1])
    re = jnp.concatenate([even[:, :quarter], odd[:, :quarter]], axis=1)
    im = jnp.concatenate([even[:, quarter:], odd[:, quarter:]], axis=1)
    power = re * re + im * im
    rows = power.shape[0]
    top, rest = split(power)
    both = dot(jnp.concatenate([top, rest], axis=0), band_ref[...])
    smooth = (both[:rows] + both[rows:]) * share_ref[...]
    factor = 1.0 / jnp.sqrt(smooth + 1e-05)
    white = jnp.concatenate([(re * factor).astype(BF16), (im * factor).astype(BF16)], axis=0)
    out_ref[...] = dot(one_hot(index_ref[...], 2 * rows), white).astype(BF16)


def select_kernel(x_ref, index_ref, own_ref, other_ref):
    rows = own_ref.shape[0]
    picked = dot(one_hot(index_ref[...], x_ref.shape[0]), x_ref[...]).astype(BF16)
    own_ref[...] = picked[:rows]
    other_ref[...] = picked[rows:]


def cross_kernel(own_ref, other_ref, out_ref):
    for block in range(2):
        base = block * 64
        homes, partners = [], []
        for ref in (own_ref, other_ref):
            for window in range(2):
                at = base + window * 16
                homes.append(ref[at : at + 16, :].astype(F32))
                partners.append(ref[at + 32 : at + 48, :].astype(F32))
        for home in range(8):
            cr = ci = 0.0
            for a, b in zip(homes, partners):
                ar, ai = a[home : home + 1], a[home + 8 : home + 9]
                br, bi = b[:8], b[8:]
                cr = cr + (ar * br + ai * bi)
                ci = ci + (ai * br - ar * bi)
            row = (block * 8 + home) * 16
            out_ref[row : row + 16, :] = jnp.concatenate([cr, ci], axis=0).astype(BF16)


def inverse_kernel(x_ref, top_ref, rest_ref, scale_ref, out_ref):
    half = x_ref.shape[1]
    quarter = half // 2
    total = x_ref[0:16, :].astype(F32)
    for source in range(1, x_ref.shape[0] // 16):
        total = total + x_ref[source * 16 : source * 16 + 16, :].astype(F32)
    cr, ci = total[:8], total[8:]
    even = jnp.concatenate([cr[:, :quarter], ci[:, :quarter]], axis=1)
    odd = jnp.concatenate([cr[:, quarter:], ci[:, quarter:]], axis=1)
    even = product(even, top_ref[0], rest_ref[0])
    odd = product(odd, top_ref[1], rest_ref[1])
    scale = scale_ref[0]
    out_ref[:, half:] = (even + odd) * scale
    out_ref[:, :half] = (even - odd) * scale


VMEM = pl.BlockSpec(memory_space=pltpu.VMEM)
SMEM = pl.BlockSpec(memory_space=pltpu.SMEM)
PARAMS = pltpu.CompilerParams(vmem_limit_bytes=40 * 1024 * 1024)


def call(kernel, out, operands, specs=None):
    outs = out if isinstance(out, tuple) else None
    return pl.pallas_call(
        kernel,
        out_shape=out,
        in_specs=specs or [VMEM] * len(operands),
        out_specs=(VMEM,) * len(outs) if outs else VMEM,
        compiler_params=PARAMS,
    )(*operands)


def shape(rows, columns, dtype=BF16):
    return jax.ShapeDtypeStruct((rows, columns), dtype)


def body(traces, needed, home_slot, partner_slot, live_blocks):
    chan_dev, win_dev, samples = traces.shape
    bins = samples // 2
    groups = lax.axis_size("chan")
    win_count = lax.axis_size("win")
    owner = lax.axis_index("chan")
    place = lax.axis_index("win")
    core = place % 2
    length = needed.shape[1]
    capacity = 2 * length // groups
    per_group = 2 * capacity * win_dev

    first = owner * chan_dev
    begin = jnp.sum((needed < first).astype(jnp.int32), axis=1)
    listing = jnp.arange(length, dtype=jnp.int32)
    slot = jnp.arange(capacity, dtype=jnp.int32)
    hit = listing[None, None, :] == begin[:, None, None] + slot[None, :, None]
    chosen = jnp.sum(jnp.where(hit, needed[:, None, :] - first, 0), axis=2)
    part = jnp.arange(2, dtype=jnp.int32)
    send_index = (
        part[None, :, None, None] * (chan_dev * win_dev)
        + chosen[:, None, :, None] * win_dev
        + part[None, None, None, :]
    ).reshape(-1, 1)

    fore_top, fore_rest = forward_tables(samples)
    band, share = band_tables(bins)
    outgoing = call(
        spectra_kernel,
        shape(groups * per_group, bins),
        (traces.reshape(chan_dev * win_dev, samples), fore_top, fore_rest, band, share, send_index),
    )
    incoming = lax.all_to_all(
        outgoing.reshape(groups, per_group, bins), "chan", split_axis=0, concat_axis=0, tiled=True
    ).reshape(groups * per_group, bins)

    listed = lax.dynamic_index_in_dim(needed, owner, 0, keepdims=False)
    source = listed // chan_dev
    start = jnp.sum((listed[None, :] < (source * chan_dev)[:, None]).astype(jnp.int32), axis=1)
    row_of = source * per_group + (listing - start) * win_dev
    two = partner_slot.reshape(2, 2, 8)
    sides = []
    for side in (core, 1 - core):
        mine = jnp.where(side == 0, two[:, 0], two[:, 1])
        sides.append(jnp.stack([home_slot, mine], axis=1))
    slots = jnp.stack(sides)
    picked = jnp.sum(jnp.where(slots[..., None] == listing, row_of, 0), axis=-1)
    pick_index = (
        picked[:, :, :, None, None, :]
        + part[:, None, None]
        + part[None, :, None] * (capacity * win_dev)
    ).reshape(-1, 1)

    own, other = call(
        select_kernel, (shape(128, bins), shape(128, bins)), (incoming, pick_index)
    )
    received = lax.ppermute(other, "win", [(i, i ^ 1) for i in range(win_count)])
    terms = call(cross_kernel, shape(256, bins), (own, received))
    same_core = [list(range(c, win_count, 2)) for c in range(2)]
    gathered = lax.all_to_all(
        terms.reshape(16, 16, bins),
        "win",
        split_axis=0,
        concat_axis=0,
        axis_index_groups=same_core,
        tiled=True,
    ).reshape(256, bins)

    back_top, back_rest = inverse_tables(samples)
    norm_scale = 1.0 / math.sqrt(samples * win_dev * win_count)
    live = (place // (win_count // 2) < live_blocks).astype(F32) * norm_scale
    return call(
        inverse_kernel,
        shape(8, samples, F32),
        (gathered, back_top, back_rest, live),
        [VMEM, VMEM, VMEM, SMEM],
    )


def solution(mesh):
    placed = (P("chan", "win", None), P(), P("chan", None), P("chan", None), P("chan"))
    return jax.shard_map(
        body, mesh=mesh, in_specs=placed, out_specs=P(("chan", "win"), None), check_vma=False
    )
```

```python
import math

import jax
import jax.numpy as jnp
import ml_dtypes
import numpy as np
from jax import lax
from jax.experimental import pallas as pl
from jax.experimental.pallas import tpu as pltpu
from jax.sharding import PartitionSpec as P

band_reach = 64
F32 = jnp.float32
BF16 = jnp.bfloat16


def halves(table):
    top = table.astype(ml_dtypes.bfloat16)
    rest = (table - top.astype(np.float64)).astype(ml_dtypes.bfloat16)
    return top, rest


def forward_tables(samples):
    n = np.arange(samples // 2)[:, None]
    parts = []
    for first in (0, 1):
        k = np.arange(first, samples // 2, 2)[None, :]
        angle = (n * k % samples) * (2.0 * math.pi / samples)
        parts.append(np.concatenate([np.cos(angle), -np.sin(angle)], axis=1))
    return halves(np.stack(parts))


def inverse_tables(samples):
    lag = np.arange(samples // 2)[None, :]
    parts = []
    for first in (0, 1):
        f = np.arange(first, samples // 2, 2)[:, None]
        angle = (f * lag % samples) * (2.0 * math.pi / samples)
        weight = np.where(f == 0, 1.0, 2.0)
        parts.append(np.concatenate([weight * np.cos(angle), -weight * np.sin(angle)], axis=0))
    return halves(np.stack(parts))


def split(x):
    top = x.astype(BF16)
    return top, (x - top.astype(F32)).astype(BF16)


def dot(a, b):
    return jnp.dot(a, b, preferred_element_type=F32)


def product(x, table_top, table_rest):
    rows = x.shape[0]
    top, rest = split(x)
    both = dot(jnp.concatenate([top, rest], axis=0), table_top)
    return both[:rows] + both[rows:] + dot(top, table_rest)


def one_hot(index, size):
    spots = lax.broadcasted_iota(jnp.int32, (index.shape[0], size), 1)
    return jnp.where(spots == index, 1.0, 0.0).astype(BF16)


def send_rows(needed, owner, channels):
    owners, length = needed.shape
    capacity = 2 * length // owners
    per_owner = 4 * capacity
    spread = jnp.concatenate(
        [jnp.broadcast_to(needed[o : o + 1], (per_owner, length)) for o in range(owners)], axis=0
    )
    offset = spread - owner * channels
    row = lax.broadcasted_iota(jnp.int32, (owners * per_owner, 1), 0)
    row = lax.rem(row, per_owner)
    part = lax.div(row, 2 * capacity)
    slot = lax.div(lax.rem(row, 2 * capacity), 2)
    window = lax.rem(row, 2)
    begin = jnp.sum(jnp.where(offset < 0, 1.0, 0.0), axis=1, keepdims=True).astype(jnp.int32)
    at = lax.broadcasted_iota(jnp.int32, spread.shape, 1)
    chosen = jnp.where(at == begin + slot, offset, 0).astype(F32)
    chosen = jnp.sum(chosen, axis=1, keepdims=True).astype(jnp.int32)
    return part * (2 * channels) + window * channels + chosen


def band_sums(freq_bins):
    half = freq_bins // 2

    def bin_of(place):
        return jnp.where(place < half, 2 * place, 2 * place - (freq_bins - 1))

    rows = bin_of(lax.broadcasted_iota(jnp.int32, (freq_bins, freq_bins), 0))
    columns = bin_of(lax.broadcasted_iota(jnp.int32, (freq_bins, freq_bins), 1))
    inside = jnp.where(jnp.abs(rows - columns) <= band_reach, 1.0, 0.0).astype(BF16)
    k = bin_of(lax.broadcasted_iota(jnp.int32, (1, freq_bins), 1))
    count = jnp.minimum(k, band_reach) + jnp.minimum(freq_bins - 1 - k, band_reach) + 1
    return inside, 1.0 / count.astype(F32)


def spectra_kernel(owner_ref, x_hbm, table_hbm, needed_hbm, out_ref, x_ref, table_ref, needed_ref, band_ref, sems):
    channels, windows, samples = x_ref.shape
    half, quarter = samples // 2, samples // 4
    copies = [pltpu.make_async_copy(needed_hbm, needed_ref, sems.at[0])]
    for i in range(2):
        part = pl.ds(i * (channels // 2), channels // 2)
        copies.append(pltpu.make_async_copy(x_hbm.at[part], x_ref.at[part], sems.at[1 + i]))
    for i in range(8):
        part = (i // 2, pl.ds(i % 2 * quarter, quarter))
        copies.append(
            pltpu.make_async_copy(table_hbm.at[part], table_ref.at[part], sems.at[3 + i])
        )
    for copy in copies:
        copy.start()

    band, share = band_sums(half)
    band_ref[...] = band
    copies[0].wait()
    chosen = one_hot(send_rows(needed_ref[...], owner_ref[0], channels), 4 * channels)
    copies[1].wait()
    copies[2].wait()
    x = jnp.concatenate([x_ref[:, w, :] for w in range(windows)], axis=0)
    rows = x.shape[0]
    left, right = x[:, :half], x[:, half:]
    spectrum = []
    for parity, side in enumerate((left + right, left - right)):
        top, rest = split(side)
        for i in range(4):
            copies[3 + parity * 4 + i].wait()
        both = dot(jnp.concatenate([top, rest], axis=0), table_ref[2 * parity])
        spectrum.append(both[:rows] + both[rows:] + dot(top, table_ref[2 * parity + 1]))
    even, odd = spectrum
    re = jnp.concatenate([even[:, :quarter], odd[:, :quarter]], axis=1)
    im = jnp.concatenate([even[:, quarter:], odd[:, quarter:]], axis=1)
    power = re * re + im * im
    top, rest = split(power)
    both = dot(jnp.concatenate([top, rest], axis=0), band_ref[...])
    smooth = (both[:rows] + both[rows:]) * share
    factor = 1.0 / jnp.sqrt(smooth + 1e-05)
    white = jnp.concatenate([(re * factor).astype(BF16), (im * factor).astype(BF16)], axis=0)
    picked = dot(chosen, white).astype(BF16)
    width = out_ref.shape[2]
    for part in range(out_ref.shape[0]):
        out_ref[part] = picked[:, part * width : (part + 1) * width]


def cross_kernel(x_ref, index_ref, out_ref, held_ref):
    parts, rows, width = x_ref.shape
    x = jnp.concatenate([x_ref[part] for part in range(parts)], axis=1)
    held_ref[...] = dot(one_hot(index_ref[...], rows), x)
    for block in range(2):
        for home in range(8):
            cr = ci = 0.0
            for window in range(2):
                re = (block * 2 + window) * 48
                im = re + 24
                for part in range(parts):
                    lanes = slice(part * width, (part + 1) * width)
                    ar = held_ref[re + home : re + home + 1, lanes]
                    ai = held_ref[im + home : im + home + 1, lanes]
                    br = held_ref[re + 8 : re + 24, lanes]
                    bi = held_ref[im + 8 : im + 24, lanes]
                    cr = cr + (ar * br + ai * bi)
                    ci = ci + (ai * br - ar * bi)
            terms = jnp.concatenate([cr[:8], ci[:8], cr[8:], ci[8:]], axis=0)
            row = (block * 8 + home) * 32
            out_ref[row : row + 32, :] = terms.astype(BF16)


def inverse_kernel(x_ref, top_ref, rest_ref, scale_ref, out_ref):
    half = out_ref.shape[1] // 2
    re, im = [], []
    for part in range(4):
        total = 0.0
        for source in range(part, x_ref.shape[0] // 16, 4):
            total = total + x_ref[source * 16 : source * 16 + 16, :].astype(F32)
        re.append(total[:8])
        im.append(total[8:])
    even = product(jnp.concatenate(re[:2] + im[:2], axis=1), top_ref[0], rest_ref[0])
    odd = product(jnp.concatenate(re[2:] + im[2:], axis=1), top_ref[1], rest_ref[1])
    scale = scale_ref[0]
    out_ref[:, half:] = (even + odd) * scale
    out_ref[:, :half] = (even - odd) * scale


VMEM = pl.BlockSpec(memory_space=pltpu.VMEM)
SMEM = pl.BlockSpec(memory_space=pltpu.SMEM)
HBM = pl.BlockSpec(memory_space=pltpu.HBM)
MIB = 1024 * 1024


def call(kernel, out, operands, specs=None, scratch=(), vmem=32 * MIB):
    return pl.pallas_call(
        kernel,
        out_shape=out,
        in_specs=specs or [VMEM] * len(operands),
        out_specs=VMEM,
        scratch_shapes=scratch,
        compiler_params=pltpu.CompilerParams(vmem_limit_bytes=vmem),
    )(*operands)


def body(traces, needed, home_slot, partner_slot, live_blocks):
    chan_dev, win_dev, samples = traces.shape
    bins = samples // 2
    groups = lax.axis_size("chan")
    win_count = lax.axis_size("win")
    owner = lax.axis_index("chan")
    place = lax.axis_index("win")
    length = needed.shape[1]
    capacity = 2 * length // groups
    per_group = 2 * capacity * win_dev
    parts = 4
    width = bins // parts

    tops, rests = forward_tables(samples)
    table = np.stack([tops[0], rests[0], tops[1], rests[1]])
    outgoing = call(
        spectra_kernel,
        jax.ShapeDtypeStruct((parts, groups * per_group, width), BF16),
        (owner[None], traces, table, needed),
        [SMEM, HBM, HBM, HBM],
        [
            pltpu.VMEM(traces.shape, F32),
            pltpu.VMEM(table.shape, BF16),
            pltpu.VMEM(needed.shape, jnp.int32),
            pltpu.VMEM((bins, bins), BF16),
            pltpu.SemaphoreType.DMA((11,)),
        ],
        vmem=62 * MIB,
    )
    near = [
        [o * win_count + w + q for q in range(parts) for o in range(groups)]
        for w in range(0, win_count, parts)
    ]
    incoming = lax.all_to_all(
        outgoing.reshape(parts * groups, per_group, width),
        ("chan", "win"),
        split_axis=0,
        concat_axis=0,
        axis_index_groups=near,
        tiled=True,
    ).reshape(parts, groups * per_group, width)

    listing = jnp.arange(length, dtype=jnp.int32)
    listed = lax.dynamic_index_in_dim(needed, owner, 0, keepdims=False)
    source = listed // chan_dev
    start = jnp.sum((listed[None, :] < (source * chan_dev)[:, None]).astype(jnp.int32), axis=1)
    row_of = source * per_group + (listing - start) * win_dev
    slots = jnp.concatenate([home_slot, partner_slot], axis=1)
    picked = jnp.sum(jnp.where(slots[..., None] == listing, row_of, 0), axis=-1)
    part = jnp.arange(2, dtype=jnp.int32)
    pick_index = (
        picked[:, None, None, :]
        + part[None, :, None, None]
        + part[None, None, :, None] * (capacity * win_dev)
    ).reshape(-1, 1)
    terms = call(
        cross_kernel,
        jax.ShapeDtypeStruct((win_count * 16, width), BF16),
        (incoming, pick_index),
        scratch=[pltpu.VMEM((pick_index.shape[0], bins), F32)],
    )
    gathered = lax.all_to_all(
        terms.reshape(win_count, 16, width), "win", split_axis=0, concat_axis=0, tiled=True
    ).reshape(win_count * 16, width)

    back_top, back_rest = inverse_tables(samples)
    norm_scale = 1.0 / math.sqrt(samples * win_dev * win_count)
    live = (place // (win_count // 2) < live_blocks).astype(F32) * norm_scale
    return call(
        inverse_kernel,
        jax.ShapeDtypeStruct((8, samples), F32),
        (gathered, back_top, back_rest, live),
        [VMEM, VMEM, VMEM, SMEM],
    )


def solution(mesh):
    placed = (P("chan", "win", None), P(), P("chan", None), P("chan", None), P("chan"))
    return jax.shard_map(
        body, mesh=mesh, in_specs=placed, out_specs=P(("chan", "win"), None), check_vma=False
    )
```

```python
import math

import jax
import jax.numpy as jnp
import ml_dtypes
import numpy as np
from jax import lax
from jax.experimental import pallas as pl
from jax.experimental.pallas import tpu as pltpu
from jax.sharding import PartitionSpec as P

band_reach = 64
first_owner = 10
first_place = 16
F32 = jnp.float32
BF16 = jnp.bfloat16


def halves(table):
    top = table.astype(ml_dtypes.bfloat16)
    rest = (table - top.astype(np.float64)).astype(ml_dtypes.bfloat16)
    return top, rest


def forward_tables(samples):
    n = np.arange(samples // 2)[:, None]
    parts = []
    for first in (0, 1):
        k = np.arange(first, samples // 2, 2)[None, :]
        angle = (n * k % samples) * (2.0 * math.pi / samples)
        parts.append(np.concatenate([np.cos(angle), -np.sin(angle)], axis=1))
    return halves(np.stack(parts))


def inverse_tables(samples):
    lag = np.arange(samples // 2)[None, :]
    parts = []
    for first in (0, 1):
        f = np.arange(first, samples // 2, 2)[:, None]
        angle = (f * lag % samples) * (2.0 * math.pi / samples)
        weight = np.where(f == 0, 1.0, 2.0)
        parts.append(np.concatenate([weight * np.cos(angle), -weight * np.sin(angle)], axis=0))
    return halves(np.stack(parts))


def split(x):
    top = x.astype(BF16)
    return top, (x - top.astype(F32)).astype(BF16)


def dot(a, b):
    return jnp.dot(a, b, preferred_element_type=F32)


def product(x, table_top, table_rest):
    rows = x.shape[0]
    top, rest = split(x)
    both = dot(jnp.concatenate([top, rest], axis=0), table_top)
    return both[:rows] + both[rows:] + dot(top, table_rest)


def one_hot(index, size):
    spots = lax.broadcasted_iota(jnp.int32, (index.shape[0], size), 1)
    return jnp.where(spots == index, 1.0, 0.0).astype(BF16)


def turned(members, first):
    members = list(members)
    return members[first:] + members[:first]


def send_rows(needed, owner, channels):
    owners, length = needed.shape
    capacity = 2 * length // owners
    per_owner = 4 * capacity
    spread = jnp.concatenate(
        [
            jnp.broadcast_to(needed[o : o + 1], (per_owner, length))
            for o in turned(range(owners), first_owner)
        ],
        axis=0,
    )
    offset = spread - owner * channels
    row = lax.broadcasted_iota(jnp.int32, (owners * per_owner, 1), 0)
    row = lax.rem(row, per_owner)
    part = lax.div(row, 2 * capacity)
    slot = lax.div(lax.rem(row, 2 * capacity), 2)
    window = lax.rem(row, 2)
    begin = jnp.sum(jnp.where(offset < 0, 1.0, 0.0), axis=1, keepdims=True).astype(jnp.int32)
    at = lax.broadcasted_iota(jnp.int32, spread.shape, 1)
    chosen = jnp.where(at == begin + slot, offset, 0).astype(F32)
    chosen = jnp.sum(chosen, axis=1, keepdims=True).astype(jnp.int32)
    return part * (2 * channels) + window * channels + chosen


def band_sums(freq_bins):
    half = freq_bins // 2

    def bin_of(place):
        return jnp.where(place < half, 2 * place, 2 * place - (freq_bins - 1))

    rows = bin_of(lax.broadcasted_iota(jnp.int32, (freq_bins, freq_bins), 0))
    columns = bin_of(lax.broadcasted_iota(jnp.int32, (freq_bins, freq_bins), 1))
    inside = jnp.where(jnp.abs(rows - columns) <= band_reach, 1.0, 0.0).astype(BF16)
    k = bin_of(lax.broadcasted_iota(jnp.int32, (1, freq_bins), 1))
    count = jnp.minimum(k, band_reach) + jnp.minimum(freq_bins - 1 - k, band_reach) + 1
    return inside, 1.0 / count.astype(F32)


def spectra_kernel(owner_ref, x_hbm, table_hbm, needed_hbm, out_ref, x_ref, table_ref, needed_ref, band_ref, sems):
    channels, windows, samples = x_ref.shape
    half, quarter = samples // 2, samples // 4
    copies = [pltpu.make_async_copy(needed_hbm, needed_ref, sems.at[0])]
    for i in range(2):
        part = pl.ds(i * (channels // 2), channels // 2)
        copies.append(pltpu.make_async_copy(x_hbm.at[part], x_ref.at[part], sems.at[1 + i]))
    for i in range(8):
        part = (i // 2, pl.ds(i % 2 * quarter, quarter))
        copies.append(
            pltpu.make_async_copy(table_hbm.at[part], table_ref.at[part], sems.at[3 + i])
        )
    for copy in copies:
        copy.start()

    band, share = band_sums(half)
    band_ref[...] = band
    copies[0].wait()
    chosen = one_hot(send_rows(needed_ref[...], owner_ref[0], channels), 4 * channels)
    copies[1].wait()
    copies[2].wait()
    x = jnp.concatenate([x_ref[:, w, :] for w in range(windows)], axis=0)
    rows = x.shape[0]
    left, right = x[:, :half], x[:, half:]
    spectrum = []
    for parity, side in enumerate((left + right, left - right)):
        top, rest = split(side)
        for i in range(4):
            copies[3 + parity * 4 + i].wait()
        both = dot(jnp.concatenate([top, rest], axis=0), table_ref[2 * parity])
        spectrum.append(both[:rows] + both[rows:] + dot(top, table_ref[2 * parity + 1]))
    even, odd = spectrum
    re = jnp.concatenate([even[:, :quarter], odd[:, :quarter]], axis=1)
    im = jnp.concatenate([even[:, quarter:], odd[:, quarter:]], axis=1)
    power = re * re + im * im
    top, rest = split(power)
    both = dot(jnp.concatenate([top, rest], axis=0), band_ref[...])
    smooth = (both[:rows] + both[rows:]) * share
    factor = 1.0 / jnp.sqrt(smooth + 1e-05)
    white = jnp.concatenate([(re * factor).astype(BF16), (im * factor).astype(BF16)], axis=0)
    picked = dot(chosen, white).astype(BF16)
    width = out_ref.shape[2]
    for part in range(out_ref.shape[0]):
        out_ref[part] = picked[:, part * width : (part + 1) * width]


def cross_kernel(x_ref, index_ref, out_ref, held_ref):
    parts, rows, width = x_ref.shape
    x = jnp.concatenate([x_ref[part] for part in range(parts)], axis=1)
    held_ref[...] = dot(one_hot(index_ref[...], rows), x)
    for block in range(2):
        for home in range(8):
            cr = ci = 0.0
            for window in range(2):
                re = (block * 2 + window) * 48
                im = re + 24
                for part in range(parts):
                    lanes = slice(part * width, (part + 1) * width)
                    ar = held_ref[re + home : re + home + 1, lanes]
                    ai = held_ref[im + home : im + home + 1, lanes]
                    br = held_ref[re + 8 : re + 24, lanes]
                    bi = held_ref[im + 8 : im + 24, lanes]
                    cr = cr + (ar * br + ai * bi)
                    ci = ci + (ai * br - ar * bi)
            terms = jnp.concatenate([cr[:8], ci[:8], cr[8:], ci[8:]], axis=0)
            row = ((block * 8 + home) * 32 - first_place * 16) % out_ref.shape[0]
            out_ref[row : row + 32, :] = terms.astype(BF16)


def inverse_kernel(x_ref, top_ref, rest_ref, scale_ref, out_ref):
    half = out_ref.shape[1] // 2
    re, im = [], []
    for part in range(4):
        total = 0.0
        for source in range(part, x_ref.shape[0] // 16, 4):
            total = total + x_ref[source * 16 : source * 16 + 16, :].astype(F32)
        re.append(total[:8])
        im.append(total[8:])
    even = product(jnp.concatenate(re[:2] + im[:2], axis=1), top_ref[0], rest_ref[0])
    odd = product(jnp.concatenate(re[2:] + im[2:], axis=1), top_ref[1], rest_ref[1])
    scale = scale_ref[0]
    out_ref[:, half:] = (even + odd) * scale
    out_ref[:, :half] = (even - odd) * scale


VMEM = pl.BlockSpec(memory_space=pltpu.VMEM)
SMEM = pl.BlockSpec(memory_space=pltpu.SMEM)
HBM = pl.BlockSpec(memory_space=pltpu.HBM)
MIB = 1024 * 1024


def call(kernel, out, operands, specs=None, scratch=(), vmem=32 * MIB):
    return pl.pallas_call(
        kernel,
        out_shape=out,
        in_specs=specs or [VMEM] * len(operands),
        out_specs=VMEM,
        scratch_shapes=scratch,
        compiler_params=pltpu.CompilerParams(vmem_limit_bytes=vmem),
    )(*operands)


def body(traces, needed, home_slot, partner_slot, live_blocks):
    chan_dev, win_dev, samples = traces.shape
    bins = samples // 2
    groups = lax.axis_size("chan")
    win_count = lax.axis_size("win")
    owner = lax.axis_index("chan")
    place = lax.axis_index("win")
    length = needed.shape[1]
    capacity = 2 * length // groups
    per_group = 2 * capacity * win_dev
    parts = 4
    width = bins // parts

    tops, rests = forward_tables(samples)
    table = np.stack([tops[0], rests[0], tops[1], rests[1]])
    outgoing = call(
        spectra_kernel,
        jax.ShapeDtypeStruct((parts, groups * per_group, width), BF16),
        (owner[None], traces, table, needed),
        [SMEM, HBM, HBM, HBM],
        [
            pltpu.VMEM(traces.shape, F32),
            pltpu.VMEM(table.shape, BF16),
            pltpu.VMEM(needed.shape, jnp.int32),
            pltpu.VMEM((bins, bins), BF16),
            pltpu.SemaphoreType.DMA((11,)),
        ],
        vmem=62 * MIB,
    )
    near = [
        [
            o * win_count + w + q
            for q in range(parts)
            for o in turned(range(groups), first_owner)
        ]
        for w in range(0, win_count, parts)
    ]
    incoming = lax.all_to_all(
        outgoing.reshape(parts * groups, per_group, width),
        ("chan", "win"),
        split_axis=0,
        concat_axis=0,
        axis_index_groups=near,
        tiled=True,
    ).reshape(parts, groups * per_group, width)

    listing = jnp.arange(length, dtype=jnp.int32)
    listed = lax.dynamic_index_in_dim(needed, owner, 0, keepdims=False)
    source = listed // chan_dev
    start = jnp.sum((listed[None, :] < (source * chan_dev)[:, None]).astype(jnp.int32), axis=1)
    turn = (source - first_owner) % groups
    row_of = turn * per_group + (listing - start) * win_dev
    slots = jnp.concatenate([home_slot, partner_slot], axis=1)
    picked = jnp.sum(jnp.where(slots[..., None] == listing, row_of, 0), axis=-1)
    part = jnp.arange(2, dtype=jnp.int32)
    pick_index = (
        picked[:, None, None, :]
        + part[None, :, None, None]
        + part[None, None, :, None] * (capacity * win_dev)
    ).reshape(-1, 1)
    terms = call(
        cross_kernel,
        jax.ShapeDtypeStruct((win_count * 16, width), BF16),
        (incoming, pick_index),
        scratch=[pltpu.VMEM((pick_index.shape[0], bins), F32)],
    )
    gathered = lax.all_to_all(
        terms.reshape(win_count, 16, width),
        "win",
        split_axis=0,
        concat_axis=0,
        axis_index_groups=[turned(range(win_count), first_place)],
        tiled=True,
    ).reshape(win_count * 16, width)

    back_top, back_rest = inverse_tables(samples)
    norm_scale = 1.0 / math.sqrt(samples * win_dev * win_count)
    live = (place // (win_count // 2) < live_blocks).astype(F32) * norm_scale
    return call(
        inverse_kernel,
        jax.ShapeDtypeStruct((8, samples), F32),
        (gathered, back_top, back_rest, live),
        [VMEM, VMEM, VMEM, SMEM],
    )


def solution(mesh):
    placed = (P("chan", "win", None), P(), P("chan", None), P("chan", None), P("chan"))
    return jax.shard_map(
        body, mesh=mesh, in_specs=placed, out_specs=P(("chan", "win"), None), check_vma=False
    )
```

```python
import math

import jax
import jax.numpy as jnp
import ml_dtypes
import numpy as np
from jax import lax
from jax.experimental import pallas as pl
from jax.experimental.pallas import tpu as pltpu
from jax.sharding import PartitionSpec as P

band_reach = 64
bin_groups = (0, 2, 1, 3)
first_owner = 10
first_place = 20
F32 = jnp.float32
BF16 = jnp.bfloat16
I32 = jnp.int32


def turned(members, first):
    members = list(members)
    return members[first:] + members[:first]


def wave_tables(samples):
    n = np.arange(samples // 4)[:, None]
    parts = []
    for first in bin_groups:
        k = np.arange(first, samples // 2, 4)[None, :]
        angle = (n * k % samples) * (2.0 * math.pi / samples)
        parts.append(np.concatenate([np.cos(angle), np.sin(angle)], axis=1))
    table = np.stack(parts)
    top = table.astype(ml_dtypes.bfloat16)
    rest = (table - top.astype(np.float64)).astype(ml_dtypes.bfloat16)
    return np.stack([top, rest])


def split(x):
    top = x.astype(BF16)
    return top, (x - top.astype(F32)).astype(BF16)


def dot(a, b):
    return jnp.dot(a, b, preferred_element_type=F32)


def dot_back(a, b):
    return lax.dot_general(a, b, (((1,), (1,)), ((), ())), preferred_element_type=F32)


def product(x, table_top, table_rest, by=dot):
    rows = x.shape[0]
    top, rest = split(x)
    both = by(jnp.concatenate([top, rest], axis=0), table_top)
    return both[:rows] + both[rows:] + by(top, table_rest)


def iota(shape, axis):
    return lax.broadcasted_iota(I32, shape, axis)


def total(x, axis):
    return jnp.sum(x.astype(F32), axis=axis, keepdims=True).astype(I32)


def one_hot(index, size):
    spots = iota((index.shape[0], size), 1)
    return jnp.where(spots == index, 1.0, 0.0).astype(BF16)


def column(row):
    n = row.shape[1]
    spread = jnp.broadcast_to(row, (n, n))
    return total(jnp.where(iota((n, n), 0) == iota((n, n), 1), spread, 0), 1)


def send_rows(needed, owner, channels):
    owners, length = needed.shape
    capacity = 2 * length // owners
    per_owner = 4 * capacity
    spread = jnp.concatenate(
        [
            jnp.broadcast_to(needed[o : o + 1], (per_owner, length))
            for o in turned(range(owners), first_owner)
        ],
        axis=0,
    )
    offset = spread - owner * channels
    row = lax.rem(iota((owners * per_owner, 1), 0), per_owner)
    part = lax.div(row, 2 * capacity)
    slot = lax.div(lax.rem(row, 2 * capacity), 2)
    window = lax.rem(row, 2)
    begin = total(jnp.where(offset < 0, 1, 0), 1)
    chosen = total(jnp.where(iota(spread.shape, 1) == begin + slot, offset, 0), 1)
    return part * (2 * channels) + window * channels + chosen


def pick_rows(listed, homes, partners, owners, channels):
    length = listed.shape[1]
    capacity = 2 * length // owners
    source = lax.div(listed, channels)
    spread = jnp.broadcast_to(column(listed), (length, length))
    start = total(jnp.where(spread < source * channels, 1, 0), 0)
    turn = lax.rem(source + (owners - first_owner), owners)
    row_of = turn * (4 * capacity) + (iota((1, length), 1) - start) * 2
    rows = []
    for block in range(2):
        slots = [column(s[block : block + 1]) for s in (homes, partners)]
        slots = jnp.concatenate(slots, axis=0)
        spots = iota((slots.shape[0], length), 1)
        picked = total(jnp.where(spots == slots, row_of, 0), 1)
        for window in range(2):
            for part in range(2):
                rows.append(picked + (window + part * 2 * capacity))
    return jnp.concatenate(rows, axis=0)


def band_sums(freq_bins):
    group = freq_bins // 4

    def bin_of(place):
        at = lax.div(place, group)
        first = jnp.where(at == 1, 2, jnp.where(at == 2, 1, at))
        return 4 * lax.rem(place, group) + first

    rows = bin_of(iota((freq_bins, 1), 0))
    columns = bin_of(iota((1, freq_bins), 1))
    inside = jnp.where(jnp.abs(rows - columns) <= band_reach, 1.0, 0.0).astype(BF16)
    count = jnp.minimum(columns, band_reach) + jnp.minimum(freq_bins - 1 - columns, band_reach) + 1
    return inside, 1.0 / count.astype(F32)


def spectra_kernel(
    owner_ref, place_ref, live_ref, x_hbm, table_hbm, needed_hbm, homes_hbm, partners_hbm,
    out_ref, table_ref, pick_ref, scale_ref,
    x_ref, needed_ref, homes_ref, partners_ref, band_ref, sems,
):
    channels, windows, samples = x_ref.shape
    quarter = samples // 4
    owners = needed_ref.shape[0]
    pairs = [
        (needed_hbm, needed_ref),
        (homes_hbm, homes_ref),
        (partners_hbm, partners_ref),
    ]
    for i in range(2):
        part = pl.ds(i * (channels // 2), channels // 2)
        pairs.append((x_hbm.at[part], x_ref.at[part]))
    for group in range(4):
        for level in range(2):
            pairs.append((table_hbm.at[level, group], table_ref.at[level, group]))
    copies = [pltpu.make_async_copy(*pair, sems.at[i]) for i, pair in enumerate(pairs)]
    for copy in copies:
        copy.start()

    band, share = band_sums(samples // 2)
    band_ref[...] = band
    for copy in copies[:3]:
        copy.wait()
    chosen = one_hot(send_rows(needed_ref[...], owner_ref[0], channels), 4 * channels)
    listed = needed_ref[pl.ds(owner_ref[0], 1), :]
    pick_ref[...] = pick_rows(listed, homes_ref[...], partners_ref[...], owners, channels)
    live = lax.div(place_ref[0], 16) < live_ref[0]
    scale = jnp.where(live, 1.0 / math.sqrt(samples * 64), 0.0)
    scale_ref[...] = jnp.full(scale_ref.shape, scale, F32)

    for copy in copies[3:]:
        copy.wait()
    x = jnp.concatenate([x_ref[:, w, :] for w in range(windows)], axis=0)
    rows = x.shape[0]
    a, b, c, d = (x[:, i * quarter : (i + 1) * quarter] for i in range(4))
    ac, bd = a + c, b + d
    turns = jnp.concatenate([a - c, b - d], axis=0)
    re, im = [], []
    for group, side in enumerate((ac + bd, ac - bd, turns, turns)):
        waves = product(side, table_ref[0, group], table_ref[1, group])
        half = waves.shape[1] // 2
        cos, sin = waves[:, :half], waves[:, half:]
        if group < 2:
            re.append(cos)
            im.append(-sin)
        elif group == 2:
            re.append(cos[:rows] - sin[rows:])
            im.append(-sin[:rows] - cos[rows:])
        else:
            re.append(cos[:rows] + sin[rows:])
            im.append(cos[rows:] - sin[:rows])
    re, im = jnp.concatenate(re, axis=1), jnp.concatenate(im, axis=1)
    power = re * re + im * im
    top, rest = split(power)
    both = dot(jnp.concatenate([top, rest], axis=0), band_ref[...])
    smooth = (both[:rows] + both[rows:]) * share
    factor = 1.0 / jnp.sqrt(smooth + 1e-05)
    white = jnp.concatenate([(re * factor).astype(BF16), (im * factor).astype(BF16)], axis=0)
    picked = dot(chosen, white).astype(BF16)
    width = out_ref.shape[2]
    for part in range(out_ref.shape[0]):
        out_ref[part] = picked[:, part * width : (part + 1) * width]


def cross_kernel(x_ref, index_ref, out_ref, held_ref):
    parts, rows, width = x_ref.shape
    x = jnp.concatenate([x_ref[part] for part in range(parts)], axis=1)
    held_ref[...] = dot(one_hot(index_ref[...], rows), x)
    for block in range(2):
        cr, ci = [0.0] * 8, [0.0] * 8
        for window in range(2):
            re = (block * 2 + window) * 48
            im = re + 24
            for part in range(parts):
                lanes = slice(part * width, (part + 1) * width)
                br = held_ref[re + 8 : re + 24, lanes]
                bi = held_ref[im + 8 : im + 24, lanes]
                for home in range(8):
                    ar = held_ref[re + home : re + home + 1, lanes]
                    ai = held_ref[im + home : im + home + 1, lanes]
                    cr[home] = cr[home] + (ar * br + ai * bi)
                    ci[home] = ci[home] + (ai * br - ar * bi)
        for home in range(8):
            r, i = cr[home], ci[home]
            terms = jnp.concatenate([r[:8], i[:8], r[8:], i[8:]], axis=0)
            row = ((block * 8 + home) * 32 - first_place * 16) % out_ref.shape[0]
            out_ref[row : row + 32, :] = terms.astype(BF16)


def inverse_kernel(x_ref, table_ref, scale_ref, out_ref):
    quarter = out_ref.shape[1] // 4
    width = x_ref.shape[1]
    waves = []
    for group in range(4):
        terms = 0.0
        for source in range(group, x_ref.shape[0] // 16, 4):
            terms = terms + x_ref[source * 16 : source * 16 + 16, :].astype(F32)
        weight = 2.0
        if group == 0:
            weight = jnp.where(iota((1, width), 1) == 0, 1.0, 2.0)
        terms = terms * weight
        cr, ci = terms[:8], terms[8:]
        side = jnp.concatenate([cr, -ci], axis=1)
        if group >= 2:
            side = jnp.concatenate([side, jnp.concatenate([ci, cr], axis=1)], axis=0)
        waves.append(product(side, table_ref[0, group], table_ref[1, group], dot_back))
    a0, a2, b1, b3 = waves
    plus, minus = a0 + a2, a0 - a2
    cos = b1[:8] + b3[:8]
    sin = b1[8:] - b3[8:]
    scale = scale_ref[0:1, 0:1]
    for i, lags in enumerate((plus - cos, minus + sin, plus + cos, minus - sin)):
        out_ref[:, i * quarter : (i + 1) * quarter] = lags * scale


VMEM = pl.BlockSpec(memory_space=pltpu.VMEM)
SMEM = pl.BlockSpec(memory_space=pltpu.SMEM)
HBM = pl.BlockSpec(memory_space=pltpu.HBM)


def call(kernel, out, operands, specs=None, scratch=()):
    return pl.pallas_call(
        kernel,
        out_shape=out,
        in_specs=specs or [VMEM] * len(operands),
        out_specs=[VMEM] * len(out) if isinstance(out, list) else VMEM,
        scratch_shapes=scratch,
        compiler_params=pltpu.CompilerParams(vmem_limit_bytes=32 * 1024 * 1024),
    )(*operands)


def body(traces, needed, home_slot, partner_slot, live_blocks):
    samples = traces.shape[2]
    bins = samples // 2
    groups = lax.axis_size("chan")
    win_count = lax.axis_size("win")
    owner = lax.axis_index("chan")
    place = lax.axis_index("win")
    per_group = 8 * needed.shape[1] // groups
    parts = 4
    width = bins // parts
    held_rows = 4 * (home_slot.size + partner_slot.size)

    table = wave_tables(samples)
    far = [
        pltpu.with_memory_space_constraint(jnp.asarray(a), pltpu.HBM)
        for a in (traces, table, needed, home_slot, partner_slot)
    ]
    outgoing, waves, pick, scale = call(
        spectra_kernel,
        [
            jax.ShapeDtypeStruct((parts, groups * per_group, width), BF16),
            jax.ShapeDtypeStruct(table.shape, BF16),
            jax.ShapeDtypeStruct((held_rows, 1), I32),
            jax.ShapeDtypeStruct((8, 128), F32),
        ],
        (owner[None], place[None], live_blocks, *far),
        [SMEM, SMEM, SMEM] + [HBM] * len(far),
        [
            pltpu.VMEM(traces.shape, F32),
            pltpu.VMEM(needed.shape, I32),
            pltpu.VMEM(home_slot.shape, I32),
            pltpu.VMEM(partner_slot.shape, I32),
            pltpu.VMEM((bins, bins), BF16),
            pltpu.SemaphoreType.DMA((13,)),
        ],
    )
    near = [
        [
            o * win_count + w + q
            for q in range(parts)
            for o in turned(range(groups), first_owner)
        ]
        for w in range(0, win_count, parts)
    ]
    incoming = lax.all_to_all(
        outgoing.reshape(parts * groups, per_group, width),
        ("chan", "win"),
        split_axis=0,
        concat_axis=0,
        axis_index_groups=near,
        tiled=True,
    ).reshape(parts, groups * per_group, width)
    terms = call(
        cross_kernel,
        jax.ShapeDtypeStruct((win_count * 16, width), BF16),
        (incoming, pick),
        scratch=[pltpu.VMEM((held_rows, bins), F32)],
    )
    gathered = lax.all_to_all(
        terms.reshape(win_count, 16, width),
        "win",
        split_axis=0,
        concat_axis=0,
        axis_index_groups=[turned(range(win_count), first_place)],
        tiled=True,
    ).reshape(win_count * 16, width)
    return call(
        inverse_kernel, jax.ShapeDtypeStruct((8, samples), F32), (gathered, waves, scale)
    )


def solution(mesh):
    placed = (P("chan", "win", None), P(), P("chan", None), P("chan", None), P("chan"))
    return jax.shard_map(
        body, mesh=mesh, in_specs=placed, out_specs=P(("chan", "win"), None), check_vma=False
    )
```

```python
import math

import jax
import jax.numpy as jnp
import ml_dtypes
import numpy as np
from jax import lax
from jax.experimental import pallas as pl
from jax.experimental.pallas import tpu as pltpu
from jax.sharding import PartitionSpec as P

band_reach = 64
bin_groups = (0, 2, 1, 3)
owner_order = tuple((10 + i) % 16 for i in range(16))
place_order = (20, 21, 2, 3, 16, 17, 30, 31, 12, 13, 26, 27, 8, 9, 22, 23, 4, 5, 18, 19, 0, 1, 14, 15, 28, 29, 10, 11, 24, 25, 6, 7)
F32 = jnp.float32
BF16 = jnp.bfloat16
I32 = jnp.int32


def wave_tables(samples):
    n = np.arange(samples // 4)[:, None]
    parts = []
    for first in bin_groups:
        k = np.arange(first, samples // 2, 4)[None, :]
        angle = (n * k % samples) * (2.0 * math.pi / samples)
        parts.append(np.concatenate([np.cos(angle), np.sin(angle)], axis=1))
    table = np.stack(parts)
    top = table.astype(ml_dtypes.bfloat16)
    rest = (table - top.astype(np.float64)).astype(ml_dtypes.bfloat16)
    return np.stack([top, rest])


def split(x):
    top = x.astype(BF16)
    return top, (x - top.astype(F32)).astype(BF16)


def dot(a, b):
    return jnp.dot(a, b, preferred_element_type=F32)


def dot_back(a, b):
    return lax.dot_general(a, b, (((1,), (1,)), ((), ())), preferred_element_type=F32)


def product(x, table_top, table_rest, by=dot):
    rows = x.shape[0]
    top, rest = split(x)
    both = by(jnp.concatenate([top, rest], axis=0), table_top)
    return both[:rows] + both[rows:] + by(top, table_rest)


def iota(shape, axis):
    return lax.broadcasted_iota(I32, shape, axis)


def total(x, axis):
    return jnp.sum(x.astype(F32), axis=axis, keepdims=True).astype(I32)


def one_hot(index, size):
    spots = iota((index.shape[0], size), 1)
    return jnp.where(spots == index, 1.0, 0.0).astype(BF16)


def column(row):
    n = row.shape[1]
    spread = jnp.broadcast_to(row, (n, n))
    return total(jnp.where(iota((n, n), 0) == iota((n, n), 1), spread, 0), 1)


def send_rows(needed, owner, channels):
    owners, length = needed.shape
    capacity = 2 * length // owners
    per_owner = 4 * capacity
    spread = jnp.concatenate(
        [
            jnp.broadcast_to(needed[o : o + 1], (per_owner, length))
            for o in owner_order
        ],
        axis=0,
    )
    offset = spread - owner * channels
    row = lax.rem(iota((owners * per_owner, 1), 0), per_owner)
    part = lax.div(row, 2 * capacity)
    slot = lax.div(lax.rem(row, 2 * capacity), 2)
    window = lax.rem(row, 2)
    begin = total(jnp.where(offset < 0, 1, 0), 1)
    chosen = total(jnp.where(iota(spread.shape, 1) == begin + slot, offset, 0), 1)
    return part * (2 * channels) + window * channels + chosen


def pick_rows(listed, homes, partners, owners, channels):
    length = listed.shape[1]
    capacity = 2 * length // owners
    source = lax.div(listed, channels)
    spread = jnp.broadcast_to(column(listed), (length, length))
    start = total(jnp.where(spread < source * channels, 1, 0), 0)
    turn = 0
    for spot, owner in enumerate(owner_order):
        turn = jnp.where(source == owner, spot, turn)
    row_of = turn * (4 * capacity) + (iota((1, length), 1) - start) * 2
    rows = []
    for block in range(2):
        slots = [column(s[block : block + 1]) for s in (homes, partners)]
        slots = jnp.concatenate(slots, axis=0)
        spots = iota((slots.shape[0], length), 1)
        picked = total(jnp.where(spots == slots, row_of, 0), 1)
        for window in range(2):
            for part in range(2):
                rows.append(picked + (window + part * 2 * capacity))
    return jnp.concatenate(rows, axis=0)


def band_sums(freq_bins):
    group = freq_bins // 4

    def bin_of(place):
        at = lax.div(place, group)
        first = jnp.where(at == 1, 2, jnp.where(at == 2, 1, at))
        return 4 * lax.rem(place, group) + first

    rows = bin_of(iota((freq_bins, 1), 0))
    columns = bin_of(iota((1, freq_bins), 1))
    inside = jnp.where(jnp.abs(rows - columns) <= band_reach, 1.0, 0.0).astype(BF16)
    count = jnp.minimum(columns, band_reach) + jnp.minimum(freq_bins - 1 - columns, band_reach) + 1
    return inside, 1.0 / count.astype(F32)


def spectra_kernel(
    owner_ref, place_ref, live_ref, x_hbm, table_hbm, needed_hbm, homes_hbm, partners_hbm,
    out_ref, table_ref, pick_ref, scale_ref,
    x_ref, needed_ref, homes_ref, partners_ref, band_ref, sems,
):
    channels, windows, samples = x_ref.shape
    quarter = samples // 4
    owners = needed_ref.shape[0]
    pairs = [
        (needed_hbm, needed_ref),
        (homes_hbm, homes_ref),
        (partners_hbm, partners_ref),
    ]
    for i in range(2):
        part = pl.ds(i * (channels // 2), channels // 2)
        pairs.append((x_hbm.at[part], x_ref.at[part]))
    for group in range(4):
        for level in range(2):
            pairs.append((table_hbm.at[level, group], table_ref.at[level, group]))
    copies = [pltpu.make_async_copy(*pair, sems.at[i]) for i, pair in enumerate(pairs)]
    for copy in copies:
        copy.start()

    band, share = band_sums(samples // 2)
    band_ref[...] = band
    for copy in copies[:3]:
        copy.wait()
    chosen = one_hot(send_rows(needed_ref[...], owner_ref[0], channels), 4 * channels)
    listed = needed_ref[pl.ds(owner_ref[0], 1), :]
    pick_ref[...] = pick_rows(listed, homes_ref[...], partners_ref[...], owners, channels)
    live = lax.div(place_ref[0], 16) < live_ref[0]
    scale = jnp.where(live, 1.0 / math.sqrt(samples * 64), 0.0)
    scale_ref[...] = jnp.full(scale_ref.shape, scale, F32)

    for copy in copies[3:]:
        copy.wait()
    x = jnp.concatenate([x_ref[:, w, :] for w in range(windows)], axis=0)
    rows = x.shape[0]
    a, b, c, d = (x[:, i * quarter : (i + 1) * quarter] for i in range(4))
    ac, bd = a + c, b + d
    turns = jnp.concatenate([a - c, b - d], axis=0)
    re, im = [], []
    for group, side in enumerate((ac + bd, ac - bd, turns, turns)):
        waves = product(side, table_ref[0, group], table_ref[1, group])
        half = waves.shape[1] // 2
        cos, sin = waves[:, :half], waves[:, half:]
        if group < 2:
            re.append(cos)
            im.append(-sin)
        elif group == 2:
            re.append(cos[:rows] - sin[rows:])
            im.append(-sin[:rows] - cos[rows:])
        else:
            re.append(cos[:rows] + sin[rows:])
            im.append(cos[rows:] - sin[:rows])
    re, im = jnp.concatenate(re, axis=1), jnp.concatenate(im, axis=1)
    power = re * re + im * im
    top, rest = split(power)
    both = dot(jnp.concatenate([top, rest], axis=0), band_ref[...])
    smooth = (both[:rows] + both[rows:]) * share
    factor = lax.rsqrt(smooth + 1e-05)
    white = jnp.concatenate([(re * factor).astype(BF16), (im * factor).astype(BF16)], axis=0)
    picked = dot(chosen, white).astype(BF16)
    width = out_ref.shape[2]
    for part in range(out_ref.shape[0]):
        out_ref[part] = picked[:, part * width : (part + 1) * width]


def cross_kernel(x_ref, index_ref, out_ref, held_ref):
    parts, rows, width = x_ref.shape
    x = jnp.concatenate([x_ref[part] for part in range(parts)], axis=1)
    held_ref[...] = dot(one_hot(index_ref[...], rows), x)
    for block in range(2):
        cr, ci = [0.0] * 8, [0.0] * 8
        for window in range(2):
            re = (block * 2 + window) * 48
            im = re + 24
            for part in range(parts):
                lanes = slice(part * width, (part + 1) * width)
                br = held_ref[re + 8 : re + 24, lanes]
                bi = held_ref[im + 8 : im + 24, lanes]
                for home in range(8):
                    ar = held_ref[re + home : re + home + 1, lanes]
                    ai = held_ref[im + home : im + home + 1, lanes]
                    cr[home] = cr[home] + (ar * br + ai * bi)
                    ci[home] = ci[home] + (ai * br - ar * bi)
        for home in range(8):
            r, i = cr[home], ci[home]
            terms = jnp.concatenate([r[:8], i[:8], r[8:], i[8:]], axis=0)
            terms = terms.astype(BF16)
            for side in range(2):
                row = place_order.index((block * 8 + home) * 2 + side) * 16
                out_ref[row : row + 16, :] = terms[side * 16 : side * 16 + 16]


def inverse_kernel(x_ref, table_ref, scale_ref, out_ref):
    quarter = out_ref.shape[1] // 4
    width = x_ref.shape[1]
    waves = []
    for group in range(4):
        terms = 0.0
        for source, place in enumerate(place_order):
            if place % 4 != group:
                continue
            terms = terms + x_ref[source * 16 : source * 16 + 16, :].astype(F32)
        weight = 2.0
        if group == 0:
            weight = jnp.where(iota((1, width), 1) == 0, 1.0, 2.0)
        terms = terms * weight
        cr, ci = terms[:8], terms[8:]
        side = jnp.concatenate([cr, -ci], axis=1)
        if group >= 2:
            side = jnp.concatenate([side, jnp.concatenate([ci, cr], axis=1)], axis=0)
        waves.append(product(side, table_ref[0, group], table_ref[1, group], dot_back))
    a0, a2, b1, b3 = waves
    plus, minus = a0 + a2, a0 - a2
    cos = b1[:8] + b3[:8]
    sin = b1[8:] - b3[8:]
    scale = scale_ref[0:1, 0:1]
    for i, lags in enumerate((plus - cos, minus + sin, plus + cos, minus - sin)):
        out_ref[:, i * quarter : (i + 1) * quarter] = lags * scale


VMEM = pl.BlockSpec(memory_space=pltpu.VMEM)
SMEM = pl.BlockSpec(memory_space=pltpu.SMEM)
HBM = pl.BlockSpec(memory_space=pltpu.HBM)


def call(kernel, out, operands, specs=None, scratch=()):
    return pl.pallas_call(
        kernel,
        out_shape=out,
        in_specs=specs or [VMEM] * len(operands),
        out_specs=[VMEM] * len(out) if isinstance(out, list) else VMEM,
        scratch_shapes=scratch,
        compiler_params=pltpu.CompilerParams(vmem_limit_bytes=32 * 1024 * 1024),
    )(*operands)


def body(traces, needed, home_slot, partner_slot, live_blocks):
    samples = traces.shape[2]
    bins = samples // 2
    groups = lax.axis_size("chan")
    win_count = lax.axis_size("win")
    owner = lax.axis_index("chan")
    place = lax.axis_index("win")
    per_group = 8 * needed.shape[1] // groups
    parts = 4
    width = bins // parts
    held_rows = 4 * (home_slot.size + partner_slot.size)

    table = wave_tables(samples)
    far = [
        pltpu.with_memory_space_constraint(jnp.asarray(a), pltpu.HBM)
        for a in (traces, table, needed, home_slot, partner_slot)
    ]
    outgoing, waves, pick, scale = call(
        spectra_kernel,
        [
            jax.ShapeDtypeStruct((parts, groups * per_group, width), BF16),
            jax.ShapeDtypeStruct(table.shape, BF16),
            jax.ShapeDtypeStruct((held_rows, 1), I32),
            jax.ShapeDtypeStruct((8, 128), F32),
        ],
        (owner[None], place[None], live_blocks, *far),
        [SMEM, SMEM, SMEM] + [HBM] * len(far),
        [
            pltpu.VMEM(traces.shape, F32),
            pltpu.VMEM(needed.shape, I32),
            pltpu.VMEM(home_slot.shape, I32),
            pltpu.VMEM(partner_slot.shape, I32),
            pltpu.VMEM((bins, bins), BF16),
            pltpu.SemaphoreType.DMA((13,)),
        ],
    )
    near = [
        [
            o * win_count + w + q
            for q in range(parts)
            for o in owner_order
        ]
        for w in range(0, win_count, parts)
    ]
    incoming = lax.all_to_all(
        outgoing.reshape(parts * groups, per_group, width),
        ("chan", "win"),
        split_axis=0,
        concat_axis=0,
        axis_index_groups=near,
        tiled=True,
    ).reshape(parts, groups * per_group, width)
    terms = call(
        cross_kernel,
        jax.ShapeDtypeStruct((win_count * 16, width), BF16),
        (incoming, pick),
        scratch=[pltpu.VMEM((held_rows, bins), F32)],
    )
    gathered = lax.all_to_all(
        terms.reshape(win_count, 16, width),
        "win",
        split_axis=0,
        concat_axis=0,
        axis_index_groups=[list(place_order)],
        tiled=True,
    ).reshape(win_count * 16, width)
    return call(
        inverse_kernel, jax.ShapeDtypeStruct((8, samples), F32), (gathered, waves, scale)
    )


def solution(mesh):
    placed = (P("chan", "win", None), P(), P("chan", None), P("chan", None), P("chan"))
    return jax.shard_map(
        body, mesh=mesh, in_specs=placed, out_specs=P(("chan", "win"), None), check_vma=False
    )
```

```python
import math

import jax
import jax.numpy as jnp
import ml_dtypes
import numpy as np
from jax import lax
from jax.experimental import pallas as pl
from jax.experimental.pallas import tpu as pltpu
from jax.sharding import PartitionSpec as P

band_reach = 64
bin_groups = (0, 2, 1, 3)
owner_order = tuple((10 + i) % 16 for i in range(16))
place_order = (20, 21, 2, 3, 16, 17, 30, 31, 12, 13, 26, 27, 8, 9, 22, 23, 4, 5, 18, 19, 0, 1, 14, 15, 28, 29, 10, 11, 24, 25, 6, 7)
F32 = jnp.float32
BF16 = jnp.bfloat16
I32 = jnp.int32


def wave_tables(samples):
    n = np.arange(samples // 4)[:, None]
    parts = []
    for first in bin_groups:
        k = np.arange(first, samples // 2, 4)[None, :]
        angle = (n * k % samples) * (2.0 * math.pi / samples)
        parts.append(np.concatenate([np.cos(angle), np.sin(angle)], axis=1))
    table = np.stack(parts)
    top = table.astype(ml_dtypes.bfloat16)
    rest = (table - top.astype(np.float64)).astype(ml_dtypes.bfloat16)
    return np.stack([top, rest])


def split(x):
    top = x.astype(BF16)
    return top, (x - top.astype(F32)).astype(BF16)


def dot(a, b):
    return jnp.dot(a, b, preferred_element_type=F32)


def product(x, table_top, table_rest):
    rows = x.shape[0]
    top, rest = split(x)
    both = dot(jnp.concatenate([top, rest], axis=0), table_top)
    return both[:rows] + both[rows:] + dot(top, table_rest)


def iota(shape, axis):
    return lax.broadcasted_iota(I32, shape, axis)


def total(x, axis):
    return jnp.sum(x.astype(F32), axis=axis, keepdims=True).astype(I32)


def one_hot(index, size):
    spots = iota((index.shape[0], size), 1)
    return jnp.where(spots == index, 1.0, 0.0).astype(BF16)


def column(row):
    n = row.shape[1]
    spread = jnp.broadcast_to(row, (n, n))
    return total(jnp.where(iota((n, n), 0) == iota((n, n), 1), spread, 0), 1)


def send_rows(needed, owner, channels):
    owners, length = needed.shape
    capacity = 2 * length // owners
    per_owner = 4 * capacity
    spread = jnp.concatenate(
        [
            jnp.broadcast_to(needed[o : o + 1], (per_owner, length))
            for o in owner_order
        ],
        axis=0,
    )
    offset = spread - owner * channels
    row = lax.rem(iota((owners * per_owner, 1), 0), per_owner)
    part = lax.div(row, 2 * capacity)
    slot = lax.div(lax.rem(row, 2 * capacity), 2)
    window = lax.rem(row, 2)
    begin = total(jnp.where(offset < 0, 1, 0), 1)
    chosen = total(jnp.where(iota(spread.shape, 1) == begin + slot, offset, 0), 1)
    return part * (2 * channels) + window * channels + chosen


def pick_rows(listed, homes, partners, owners, channels):
    length = listed.shape[1]
    capacity = 2 * length // owners
    source = lax.div(listed, channels)
    spread = jnp.broadcast_to(column(listed), (length, length))
    start = total(jnp.where(spread < source * channels, 1, 0), 0)
    turn = 0
    for spot, owner in enumerate(owner_order):
        turn = jnp.where(source == owner, spot, turn)
    row_of = turn * (4 * capacity) + (iota((1, length), 1) - start) * 2
    rows = []
    for block in range(2):
        slots = [column(s[block : block + 1]) for s in (homes, partners)]
        slots = jnp.concatenate(slots, axis=0)
        spots = iota((slots.shape[0], length), 1)
        picked = total(jnp.where(spots == slots, row_of, 0), 1)
        for window in range(2):
            for part in range(2):
                rows.append(picked + (window + part * 2 * capacity))
    return jnp.concatenate(rows, axis=0)


def band_sums(freq_bins):
    group = freq_bins // 4

    def bin_of(place):
        at = lax.div(place, group)
        first = jnp.where(at == 1, 2, jnp.where(at == 2, 1, at))
        return 4 * lax.rem(place, group) + first

    rows = bin_of(iota((freq_bins, 1), 0))
    columns = bin_of(iota((1, freq_bins), 1))
    inside = jnp.where(jnp.abs(rows - columns) <= band_reach, 1.0, 0.0).astype(BF16)
    count = jnp.minimum(columns, band_reach) + jnp.minimum(freq_bins - 1 - columns, band_reach) + 1
    return inside, 1.0 / count.astype(F32)


def spectra_kernel(
    owner_ref, place_ref, live_ref, x_hbm, table_hbm, back_hbm, needed_hbm, homes_hbm, partners_hbm,
    out_ref, back_ref, pick_ref, scale_ref,
    x_ref, table_ref, needed_ref, homes_ref, partners_ref, band_ref, sems,
):
    channels, windows, samples = x_ref.shape
    quarter = samples // 4
    owners = needed_ref.shape[0]
    pairs = [
        (needed_hbm, needed_ref),
        (homes_hbm, homes_ref),
        (partners_hbm, partners_ref),
    ]
    for i in range(2):
        part = pl.ds(i * (channels // 2), channels // 2)
        pairs.append((x_hbm.at[part], x_ref.at[part]))
    for group in range(4):
        for level in range(2):
            pairs.append((table_hbm.at[level, group], table_ref.at[level, group]))
    last = len(pairs)
    for level in range(2):
        pairs.append((back_hbm.at[level], back_ref.at[level]))
    copies = [pltpu.make_async_copy(*pair, sems.at[i]) for i, pair in enumerate(pairs)]
    for copy in copies:
        copy.start()

    band, share = band_sums(samples // 2)
    band_ref[...] = band
    for copy in copies[:3]:
        copy.wait()
    chosen = one_hot(send_rows(needed_ref[...], owner_ref[0], channels), 4 * channels)
    listed = needed_ref[pl.ds(owner_ref[0], 1), :]
    picks = pick_rows(listed, homes_ref[...], partners_ref[...], owners, channels)
    pick_ref[...] = one_hot(picks, pick_ref.shape[1])
    live = lax.div(place_ref[0], 16) < live_ref[0]
    scale = jnp.where(live, 1.0 / math.sqrt(samples * 64), 0.0)
    scale_ref[...] = jnp.full(scale_ref.shape, scale, F32)

    for copy in copies[3:last]:
        copy.wait()
    x = jnp.concatenate([x_ref[:, w, :] for w in range(windows)], axis=0)
    rows = x.shape[0]
    a, b, c, d = (x[:, i * quarter : (i + 1) * quarter] for i in range(4))
    ac, bd = a + c, b + d
    turns = jnp.concatenate([a - c, b - d], axis=0)
    re, im = [], []
    for group, side in enumerate((ac + bd, ac - bd, turns, turns)):
        waves = product(side, table_ref[0, group], table_ref[1, group])
        half = waves.shape[1] // 2
        cos, sin = waves[:, :half], waves[:, half:]
        if group < 2:
            re.append(cos)
            im.append(-sin)
        elif group == 2:
            re.append(cos[:rows] - sin[rows:])
            im.append(-sin[:rows] - cos[rows:])
        else:
            re.append(cos[:rows] + sin[rows:])
            im.append(cos[rows:] - sin[:rows])
    re, im = jnp.concatenate(re, axis=1), jnp.concatenate(im, axis=1)
    power = re * re + im * im
    top, rest = split(power)
    both = dot(jnp.concatenate([top, rest], axis=0), band_ref[...])
    smooth = (both[:rows] + both[rows:]) * share
    factor = lax.rsqrt(smooth + 1e-05)
    white = jnp.concatenate([(re * factor).astype(BF16), (im * factor).astype(BF16)], axis=0)
    picked = dot(chosen, white).astype(BF16)
    width = out_ref.shape[2]
    for part in range(out_ref.shape[0]):
        out_ref[part] = picked[:, part * width : (part + 1) * width]
    for copy in copies[last:]:
        copy.wait()


def cross_kernel(x_ref, pick_ref, out_ref, held_ref):
    parts, _, width = x_ref.shape
    for part in range(parts):
        held_ref[:, part * width : (part + 1) * width] = dot(pick_ref[...], x_ref[part])
    for block in range(2):
        cr, ci = [0.0] * 8, [0.0] * 8
        for window in range(2):
            re = (block * 2 + window) * 48
            im = re + 24
            for part in range(parts):
                lanes = slice(part * width, (part + 1) * width)
                br = held_ref[re + 8 : re + 24, lanes]
                bi = held_ref[im + 8 : im + 24, lanes]
                for home in range(8):
                    ar = held_ref[re + home : re + home + 1, lanes]
                    ai = held_ref[im + home : im + home + 1, lanes]
                    cr[home] = cr[home] + (ar * br + ai * bi)
                    ci[home] = ci[home] + (ai * br - ar * bi)
        for home in range(8):
            r, i = cr[home], ci[home]
            terms = jnp.concatenate([r[:8], i[:8], r[8:], i[8:]], axis=0)
            terms = terms.astype(BF16)
            for side in range(2):
                row = place_order.index((block * 8 + home) * 2 + side) * 16
                out_ref[row : row + 16, :] = terms[side * 16 : side * 16 + 16]


def inverse_kernel(x_ref, table_ref, scale_ref, out_ref):
    quarter = out_ref.shape[1] // 4
    width = x_ref.shape[1]
    waves = []
    for group in range(4):
        terms = 0.0
        for source, place in enumerate(place_order):
            if place % 4 != group:
                continue
            terms = terms + x_ref[source * 16 : source * 16 + 16, :].astype(F32)
        weight = 2.0
        if group == 0:
            weight = jnp.where(iota((1, width), 1) == 0, 1.0, 2.0)
        terms = terms * weight
        cr, ci = terms[:8], terms[8:]
        side = jnp.concatenate([cr, -ci], axis=1)
        if group >= 2:
            side = jnp.concatenate([side, jnp.concatenate([ci, cr], axis=1)], axis=0)
        waves.append(product(side, table_ref[0, group], table_ref[1, group]))
    a0, a2, b1, b3 = waves
    plus, minus = a0 + a2, a0 - a2
    cos = b1[:8] + b3[:8]
    sin = b1[8:] - b3[8:]
    scale = scale_ref[0:1, 0:1]
    for i, lags in enumerate((plus - cos, minus + sin, plus + cos, minus - sin)):
        out_ref[:, i * quarter : (i + 1) * quarter] = lags * scale


VMEM = pl.BlockSpec(memory_space=pltpu.VMEM)
SMEM = pl.BlockSpec(memory_space=pltpu.SMEM)
HBM = pl.BlockSpec(memory_space=pltpu.HBM)


def call(kernel, out, operands, specs=None, scratch=()):
    return pl.pallas_call(
        kernel,
        out_shape=out,
        in_specs=specs or [VMEM] * len(operands),
        out_specs=[VMEM] * len(out) if isinstance(out, list) else VMEM,
        scratch_shapes=scratch,
        compiler_params=pltpu.CompilerParams(vmem_limit_bytes=32 * 1024 * 1024),
    )(*operands)


def body(traces, needed, home_slot, partner_slot, live_blocks):
    samples = traces.shape[2]
    bins = samples // 2
    groups = lax.axis_size("chan")
    win_count = lax.axis_size("win")
    owner = lax.axis_index("chan")
    place = lax.axis_index("win")
    per_group = 8 * needed.shape[1] // groups
    parts = 4
    width = bins // parts
    held_rows = 4 * (home_slot.size + partner_slot.size)

    table = wave_tables(samples)
    far = [
        pltpu.with_memory_space_constraint(jnp.asarray(a), pltpu.HBM)
        for a in (traces, table, table.swapaxes(2, 3), needed, home_slot, partner_slot)
    ]
    outgoing, waves, pick, scale = call(
        spectra_kernel,
        [
            jax.ShapeDtypeStruct((parts, groups * per_group, width), BF16),
            jax.ShapeDtypeStruct(table.shape, BF16),
            jax.ShapeDtypeStruct((held_rows, groups * per_group), BF16),
            jax.ShapeDtypeStruct((8, 128), F32),
        ],
        (owner[None], place[None], live_blocks, *far),
        [SMEM, SMEM, SMEM] + [HBM] * len(far),
        [
            pltpu.VMEM(traces.shape, F32),
            pltpu.VMEM(table.shape, BF16),
            pltpu.VMEM(needed.shape, I32),
            pltpu.VMEM(home_slot.shape, I32),
            pltpu.VMEM(partner_slot.shape, I32),
            pltpu.VMEM((bins, bins), BF16),
            pltpu.SemaphoreType.DMA((15,)),
        ],
    )
    near = [
        [
            o * win_count + w + q
            for q in range(parts)
            for o in owner_order
        ]
        for w in range(0, win_count, parts)
    ]
    incoming = lax.all_to_all(
        outgoing.reshape(parts * groups, per_group, width),
        ("chan", "win"),
        split_axis=0,
        concat_axis=0,
        axis_index_groups=near,
        tiled=True,
    ).reshape(parts, groups * per_group, width)
    terms = call(
        cross_kernel,
        jax.ShapeDtypeStruct((win_count * 16, width), BF16),
        (incoming, pick),
        scratch=[pltpu.VMEM((held_rows, bins), F32)],
    )
    gathered = lax.all_to_all(
        terms.reshape(win_count, 16, width),
        "win",
        split_axis=0,
        concat_axis=0,
        axis_index_groups=[list(place_order)],
        tiled=True,
    ).reshape(win_count * 16, width)
    return call(
        inverse_kernel, jax.ShapeDtypeStruct((8, samples), F32), (gathered, waves, scale)
    )


def solution(mesh):
    placed = (P("chan", "win", None), P(), P("chan", None), P("chan", None), P("chan"))
    return jax.shard_map(
        body, mesh=mesh, in_specs=placed, out_specs=P(("chan", "win"), None), check_vma=False
    )
```

```python
import math

import jax
import jax.numpy as jnp
import ml_dtypes
import numpy as np
from jax import lax
from jax.experimental import pallas as pl
from jax.experimental.pallas import tpu as pltpu
from jax.sharding import PartitionSpec as P

band_reach = 64
bin_groups = (0, 2, 1, 3)
owner_order = tuple((10 + i) % 16 for i in range(16))
quarter_order = (1, 0, 3, 2)
place_order = (20, 21, 2, 3, 16, 17, 30, 31, 12, 13, 26, 27, 8, 9, 22, 23, 4, 5, 18, 19, 0, 1, 14, 15, 28, 29, 10, 11, 24, 25, 6, 7)
F32 = jnp.float32
BF16 = jnp.bfloat16
I32 = jnp.int32


def wave_tables(samples):
    n = np.arange(samples // 4)[:, None]
    parts = []
    for first in bin_groups:
        k = np.arange(first, samples // 2, 4)[None, :]
        angle = (n * k % samples) * (2.0 * math.pi / samples)
        parts.append(np.concatenate([np.cos(angle), np.sin(angle)], axis=1))
    table = np.stack(parts)
    top = table.astype(ml_dtypes.bfloat16)
    rest = (table - top.astype(np.float64)).astype(ml_dtypes.bfloat16)
    return np.stack([top, rest])


def split(x):
    top = x.astype(BF16)
    return top, (x - top.astype(F32)).astype(BF16)


def dot(a, b):
    return jnp.dot(a, b, preferred_element_type=F32)


def product(x, table_top, table_rest):
    rows = x.shape[0]
    top, rest = split(x)
    both = dot(jnp.concatenate([top, rest], axis=0), table_top)
    return both[:rows] + both[rows:] + dot(top, table_rest)


def iota(shape, axis):
    return lax.broadcasted_iota(I32, shape, axis)


def total(x, axis):
    return jnp.sum(x.astype(F32), axis=axis, keepdims=True).astype(I32)


def one_hot(index, size):
    spots = iota((index.shape[0], size), 1)
    return jnp.where(spots == index, 1.0, 0.0).astype(BF16)


def column(row):
    n = row.shape[1]
    spread = jnp.broadcast_to(row, (n, n))
    return total(jnp.where(iota((n, n), 0) == iota((n, n), 1), spread, 0), 1)


def send_rows(needed, owner, channels):
    owners, length = needed.shape
    capacity = 2 * length // owners
    per_owner = 4 * capacity
    spread = jnp.concatenate(
        [
            jnp.broadcast_to(needed[o : o + 1], (per_owner, length))
            for o in owner_order
        ],
        axis=0,
    )
    offset = spread - owner * channels
    row = lax.rem(iota((owners * per_owner, 1), 0), per_owner)
    part = lax.div(row, 2 * capacity)
    slot = lax.div(lax.rem(row, 2 * capacity), 2)
    window = lax.rem(row, 2)
    begin = total(jnp.where(offset < 0, 1, 0), 1)
    chosen = total(jnp.where(iota(spread.shape, 1) == begin + slot, offset, 0), 1)
    return part * (2 * channels) + window * channels + chosen


def pick_rows(listed, homes, partners, owners, channels):
    length = listed.shape[1]
    capacity = 2 * length // owners
    source = lax.div(listed, channels)
    spread = jnp.broadcast_to(column(listed), (length, length))
    start = total(jnp.where(spread < source * channels, 1, 0), 0)
    turn = 0
    for spot, owner in enumerate(owner_order):
        turn = jnp.where(source == owner, spot, turn)
    row_of = turn * (4 * capacity) + (iota((1, length), 1) - start) * 2
    rows = []
    for block in range(2):
        slots = [column(s[block : block + 1]) for s in (homes, partners)]
        slots = jnp.concatenate(slots, axis=0)
        spots = iota((slots.shape[0], length), 1)
        picked = total(jnp.where(spots == slots, row_of, 0), 1)
        for window in range(2):
            for part in range(2):
                rows.append(picked + (window + part * 2 * capacity))
    return jnp.concatenate(rows, axis=0)


def band_sums(freq_bins):
    group = freq_bins // 4

    def bin_of(place):
        at = lax.div(place, group)
        first = jnp.where(at == 1, 2, jnp.where(at == 2, 1, at))
        return 4 * lax.rem(place, group) + first

    rows = bin_of(iota((freq_bins, 1), 0))
    columns = bin_of(iota((1, freq_bins), 1))
    inside = jnp.where(jnp.abs(rows - columns) <= band_reach, 1.0, 0.0).astype(BF16)
    count = jnp.minimum(columns, band_reach) + jnp.minimum(freq_bins - 1 - columns, band_reach) + 1
    return inside, 1.0 / count.astype(F32)


def spectra_kernel(
    owner_ref, place_ref, live_ref, x_hbm, table_hbm, back_hbm, needed_hbm, homes_hbm, partners_hbm,
    out_ref, back_ref, pick_ref, scale_ref,
    x_ref, table_ref, needed_ref, homes_ref, partners_ref, band_ref, sems,
):
    channels, windows, samples = x_ref.shape
    quarter = samples // 4
    owners = needed_ref.shape[0]
    pairs = [
        (needed_hbm, needed_ref),
        (homes_hbm, homes_ref),
        (partners_hbm, partners_ref),
    ]
    for i in range(2):
        part = pl.ds(i * (channels // 2), channels // 2)
        pairs.append((x_hbm.at[part], x_ref.at[part]))
    for group in range(4):
        for level in range(2):
            pairs.append((table_hbm.at[level, group], table_ref.at[level, group]))
    last = len(pairs)
    for level in range(2):
        pairs.append((back_hbm.at[level], back_ref.at[level]))
    copies = [pltpu.make_async_copy(*pair, sems.at[i]) for i, pair in enumerate(pairs)]
    for copy in copies:
        copy.start()

    band, share = band_sums(samples // 2)
    band_ref[...] = band
    for copy in copies[:3]:
        copy.wait()
    chosen = one_hot(send_rows(needed_ref[...], owner_ref[0], channels), 4 * channels)
    listed = needed_ref[pl.ds(owner_ref[0], 1), :]
    picks = pick_rows(listed, homes_ref[...], partners_ref[...], owners, channels)
    pick_ref[...] = one_hot(picks, pick_ref.shape[1])
    live = lax.div(place_ref[0], 16) < live_ref[0]
    scale = jnp.where(live, 1.0 / math.sqrt(samples * 64), 0.0)
    scale_ref[...] = jnp.full(scale_ref.shape, scale, F32)

    for copy in copies[3:last]:
        copy.wait()
    x = jnp.concatenate([x_ref[:, w, :] for w in range(windows)], axis=0)
    rows = x.shape[0]
    a, b, c, d = (x[:, i * quarter : (i + 1) * quarter] for i in range(4))
    ac, bd = a + c, b + d
    turns = jnp.concatenate([a - c, b - d], axis=0)
    re, im = [], []
    for group, side in enumerate((ac + bd, ac - bd, turns, turns)):
        waves = product(side, table_ref[0, group], table_ref[1, group])
        half = waves.shape[1] // 2
        cos, sin = waves[:, :half], waves[:, half:]
        if group < 2:
            re.append(cos)
            im.append(-sin)
        elif group == 2:
            re.append(cos[:rows] - sin[rows:])
            im.append(-sin[:rows] - cos[rows:])
        else:
            re.append(cos[:rows] + sin[rows:])
            im.append(cos[rows:] - sin[:rows])
    re, im = jnp.concatenate(re, axis=1), jnp.concatenate(im, axis=1)
    power = re * re + im * im
    top, rest = split(power)
    both = dot(jnp.concatenate([top, rest], axis=0), band_ref[...])
    smooth = (both[:rows] + both[rows:]) * share
    factor = lax.rsqrt(smooth + 1e-05)
    white = jnp.concatenate([(re * factor).astype(BF16), (im * factor).astype(BF16)], axis=0)
    picked = dot(chosen, white).astype(BF16)
    width = out_ref.shape[2]
    for spot, part in enumerate(quarter_order):
        out_ref[spot] = picked[:, part * width : (part + 1) * width]
    for copy in copies[last:]:
        copy.wait()


def cross_kernel(x_ref, pick_ref, out_ref, held_ref):
    parts, _, width = x_ref.shape
    for part in range(parts):
        held_ref[:, part * width : (part + 1) * width] = dot(pick_ref[...], x_ref[part])
    for block in range(2):
        cr, ci = [0.0] * 8, [0.0] * 8
        for window in range(2):
            re = (block * 2 + window) * 48
            im = re + 24
            for part in range(parts):
                lanes = slice(part * width, (part + 1) * width)
                br = held_ref[re + 8 : re + 24, lanes]
                bi = held_ref[im + 8 : im + 24, lanes]
                for home in range(8):
                    ar = held_ref[re + home : re + home + 1, lanes]
                    ai = held_ref[im + home : im + home + 1, lanes]
                    cr[home] = cr[home] + (ar * br + ai * bi)
                    ci[home] = ci[home] + (ai * br - ar * bi)
        for home in range(8):
            r, i = cr[home], ci[home]
            terms = jnp.concatenate([r[:8], i[:8], r[8:], i[8:]], axis=0)
            terms = terms.astype(BF16)
            for side in range(2):
                row = place_order.index((block * 8 + home) * 2 + side) * 16
                out_ref[row : row + 16, :] = terms[side * 16 : side * 16 + 16]


def inverse_kernel(x_ref, table_ref, scale_ref, out_ref):
    quarter = out_ref.shape[1] // 4
    width = x_ref.shape[1]
    waves = []
    for group in range(4):
        terms = 0.0
        for source, place in enumerate(place_order):
            if place % 4 != group:
                continue
            terms = terms + x_ref[source * 16 : source * 16 + 16, :].astype(F32)
        weight = 2.0
        if group == 0:
            weight = jnp.where(iota((1, width), 1) == 0, 1.0, 2.0)
        terms = terms * weight
        cr, ci = terms[:8], terms[8:]
        side = jnp.concatenate([cr, -ci], axis=1)
        if group >= 2:
            side = jnp.concatenate([side, jnp.concatenate([ci, cr], axis=1)], axis=0)
        waves.append(product(side, table_ref[0, group], table_ref[1, group]))
    a0, a2, b1, b3 = waves
    plus, minus = a0 + a2, a0 - a2
    cos = b1[:8] + b3[:8]
    sin = b1[8:] - b3[8:]
    scale = scale_ref[0:1, 0:1]
    for i, lags in enumerate((plus - cos, minus + sin, plus + cos, minus - sin)):
        out_ref[:, i * quarter : (i + 1) * quarter] = lags * scale


VMEM = pl.BlockSpec(memory_space=pltpu.VMEM)
SMEM = pl.BlockSpec(memory_space=pltpu.SMEM)
HBM = pl.BlockSpec(memory_space=pltpu.HBM)


def call(kernel, out, operands, specs=None, scratch=()):
    return pl.pallas_call(
        kernel,
        out_shape=out,
        in_specs=specs or [VMEM] * len(operands),
        out_specs=[VMEM] * len(out) if isinstance(out, list) else VMEM,
        scratch_shapes=scratch,
        compiler_params=pltpu.CompilerParams(vmem_limit_bytes=32 * 1024 * 1024),
    )(*operands)


def body(traces, needed, home_slot, partner_slot, live_blocks):
    samples = traces.shape[2]
    bins = samples // 2
    groups = lax.axis_size("chan")
    win_count = lax.axis_size("win")
    owner = lax.axis_index("chan")
    place = lax.axis_index("win")
    per_group = 8 * needed.shape[1] // groups
    parts = 4
    width = bins // parts
    held_rows = 4 * (home_slot.size + partner_slot.size)

    table = wave_tables(samples)
    far = [
        pltpu.with_memory_space_constraint(jnp.asarray(a), pltpu.HBM)
        for a in (traces, table, table.swapaxes(2, 3), needed, home_slot, partner_slot)
    ]
    outgoing, waves, pick, scale = call(
        spectra_kernel,
        [
            jax.ShapeDtypeStruct((parts, groups * per_group, width), BF16),
            jax.ShapeDtypeStruct(table.shape, BF16),
            jax.ShapeDtypeStruct((held_rows, groups * per_group), BF16),
            jax.ShapeDtypeStruct((8, 128), F32),
        ],
        (owner[None], place[None], live_blocks, *far),
        [SMEM, SMEM, SMEM] + [HBM] * len(far),
        [
            pltpu.VMEM(traces.shape, F32),
            pltpu.VMEM(table.shape, BF16),
            pltpu.VMEM(needed.shape, I32),
            pltpu.VMEM(home_slot.shape, I32),
            pltpu.VMEM(partner_slot.shape, I32),
            pltpu.VMEM((bins, bins), BF16),
            pltpu.SemaphoreType.DMA((15,)),
        ],
    )
    near = [
        [
            o * win_count + w + q
            for q in quarter_order
            for o in owner_order
        ]
        for w in range(0, win_count, parts)
    ]
    incoming = lax.all_to_all(
        outgoing.reshape(parts * groups, per_group, width),
        ("chan", "win"),
        split_axis=0,
        concat_axis=0,
        axis_index_groups=near,
        tiled=True,
    ).reshape(parts, groups * per_group, width)
    terms = call(
        cross_kernel,
        jax.ShapeDtypeStruct((win_count * 16, width), BF16),
        (incoming, pick),
        scratch=[pltpu.VMEM((held_rows, bins), F32)],
    )
    gathered = lax.all_to_all(
        terms.reshape(win_count, 16, width),
        "win",
        split_axis=0,
        concat_axis=0,
        axis_index_groups=[list(place_order)],
        tiled=True,
    ).reshape(win_count * 16, width)
    return call(
        inverse_kernel, jax.ShapeDtypeStruct((8, samples), F32), (gathered, waves, scale)
    )


def solution(mesh):
    placed = (P("chan", "win", None), P(), P("chan", None), P("chan", None), P("chan"))
    return jax.shard_map(
        body, mesh=mesh, in_specs=placed, out_specs=P(("chan", "win"), None), check_vma=False
    )
```

```python
import math

import jax
import jax.numpy as jnp
import ml_dtypes
import numpy as np
from jax import lax
from jax.experimental import pallas as pl
from jax.experimental.pallas import tpu as pltpu
from jax.sharding import PartitionSpec as P

band_reach = 64
bin_groups = (0, 2, 1, 3)
owner_order = tuple((10 + 7 * i) % 16 for i in range(16))
quarter_order = (1, 0, 3, 2)
place_order = (20, 21, 2, 3, 16, 17, 30, 31, 12, 13, 26, 27, 8, 9, 22, 23, 4, 5, 18, 19, 0, 1, 14, 15, 28, 29, 10, 11, 24, 25, 6, 7)
F32 = jnp.float32
BF16 = jnp.bfloat16
I32 = jnp.int32


def wave_tables(samples):
    n = np.arange(samples // 4)[:, None]
    parts = []
    for first in bin_groups:
        k = np.arange(first, samples // 2, 4)[None, :]
        angle = (n * k % samples) * (2.0 * math.pi / samples)
        parts.append(np.concatenate([np.cos(angle), np.sin(angle)], axis=1))
    table = np.stack(parts)
    top = table.astype(ml_dtypes.bfloat16)
    rest = (table - top.astype(np.float64)).astype(ml_dtypes.bfloat16)
    return np.stack([top, rest])


def split(x):
    top = x.astype(BF16)
    return top, (x - top.astype(F32)).astype(BF16)


def dot(a, b):
    return jnp.dot(a, b, preferred_element_type=F32)


def product(x, table_top, table_rest):
    rows = x.shape[0]
    top, rest = split(x)
    both = dot(jnp.concatenate([top, rest], axis=0), table_top)
    return both[:rows] + both[rows:] + dot(top, table_rest)


def iota(shape, axis):
    return lax.broadcasted_iota(I32, shape, axis)


def total(x, axis):
    return jnp.sum(x.astype(F32), axis=axis, keepdims=True).astype(I32)


def one_hot(index, size):
    spots = iota((index.shape[0], size), 1)
    return jnp.where(spots == index, 1.0, 0.0).astype(BF16)


def column(row):
    n = row.shape[1]
    spread = jnp.broadcast_to(row, (n, n))
    return total(jnp.where(iota((n, n), 0) == iota((n, n), 1), spread, 0), 1)


def send_rows(needed, owner, channels):
    owners, length = needed.shape
    capacity = 2 * length // owners
    per_owner = 4 * capacity
    spread = jnp.concatenate(
        [
            jnp.broadcast_to(needed[o : o + 1], (per_owner, length))
            for o in owner_order
        ],
        axis=0,
    )
    offset = spread - owner * channels
    row = lax.rem(iota((owners * per_owner, 1), 0), per_owner)
    part = lax.div(row, 2 * capacity)
    slot = lax.div(lax.rem(row, 2 * capacity), 2)
    window = lax.rem(row, 2)
    begin = total(jnp.where(offset < 0, 1, 0), 1)
    chosen = total(jnp.where(iota(spread.shape, 1) == begin + slot, offset, 0), 1)
    return part * (2 * channels) + window * channels + chosen


def pick_rows(listed, homes, partners, owners, channels):
    length = listed.shape[1]
    capacity = 2 * length // owners
    source = lax.div(listed, channels)
    spread = jnp.broadcast_to(column(listed), (length, length))
    start = total(jnp.where(spread < source * channels, 1, 0), 0)
    turn = 0
    for spot, owner in enumerate(owner_order):
        turn = jnp.where(source == owner, spot, turn)
    row_of = turn * (4 * capacity) + (iota((1, length), 1) - start) * 2
    rows = []
    for block in range(2):
        slots = [column(s[block : block + 1]) for s in (homes, partners)]
        slots = jnp.concatenate(slots, axis=0)
        spots = iota((slots.shape[0], length), 1)
        picked = total(jnp.where(spots == slots, row_of, 0), 1)
        for window in range(2):
            for part in range(2):
                rows.append(picked + (window + part * 2 * capacity))
    return jnp.concatenate(rows, axis=0)


def band_sums(freq_bins):
    group = freq_bins // 4

    def bin_of(place):
        at = lax.div(place, group)
        first = jnp.where(at == 1, 2, jnp.where(at == 2, 1, at))
        return 4 * lax.rem(place, group) + first

    rows = bin_of(iota((freq_bins, 1), 0))
    columns = bin_of(iota((1, freq_bins), 1))
    inside = jnp.where(jnp.abs(rows - columns) <= band_reach, 1.0, 0.0).astype(BF16)
    count = jnp.minimum(columns, band_reach) + jnp.minimum(freq_bins - 1 - columns, band_reach) + 1
    return inside, 1.0 / count.astype(F32)


def spectra_kernel(
    owner_ref, place_ref, live_ref, x_hbm, table_hbm, back_hbm, needed_hbm, homes_hbm, partners_hbm,
    out_ref, back_ref, pick_ref, scale_ref,
    x_ref, table_ref, needed_ref, homes_ref, partners_ref, band_ref, sems,
):
    channels, windows, samples = x_ref.shape
    quarter = samples // 4
    owners = needed_ref.shape[0]
    pairs = [
        (needed_hbm, needed_ref),
        (homes_hbm, homes_ref),
        (partners_hbm, partners_ref),
    ]
    for i in range(2):
        part = pl.ds(i * (channels // 2), channels // 2)
        pairs.append((x_hbm.at[part], x_ref.at[part]))
    for group in range(4):
        for level in range(2):
            pairs.append((table_hbm.at[level, group], table_ref.at[level, group]))
    last = len(pairs)
    for level in range(2):
        pairs.append((back_hbm.at[level], back_ref.at[level]))
    copies = [pltpu.make_async_copy(*pair, sems.at[i]) for i, pair in enumerate(pairs)]
    for copy in copies:
        copy.start()

    band, share = band_sums(samples // 2)
    band_ref[...] = band
    for copy in copies[:3]:
        copy.wait()
    chosen = one_hot(send_rows(needed_ref[...], owner_ref[0], channels), 4 * channels)
    listed = needed_ref[pl.ds(owner_ref[0], 1), :]
    picks = pick_rows(listed, homes_ref[...], partners_ref[...], owners, channels)
    pick_ref[...] = one_hot(picks, pick_ref.shape[1])
    live = lax.div(place_ref[0], 16) < live_ref[0]
    scale = jnp.where(live, 1.0 / math.sqrt(samples * 64), 0.0)
    scale_ref[...] = jnp.full(scale_ref.shape, scale, F32)

    for copy in copies[3:last]:
        copy.wait()
    x = jnp.concatenate([x_ref[:, w, :] for w in range(windows)], axis=0)
    rows = x.shape[0]
    a, b, c, d = (x[:, i * quarter : (i + 1) * quarter] for i in range(4))
    ac, bd = a + c, b + d
    turns = jnp.concatenate([a - c, b - d], axis=0)
    re, im = [], []
    for group, side in enumerate((ac + bd, ac - bd, turns, turns)):
        waves = product(side, table_ref[0, group], table_ref[1, group])
        half = waves.shape[1] // 2
        cos, sin = waves[:, :half], waves[:, half:]
        if group < 2:
            re.append(cos)
            im.append(-sin)
        elif group == 2:
            re.append(cos[:rows] - sin[rows:])
            im.append(-sin[:rows] - cos[rows:])
        else:
            re.append(cos[:rows] + sin[rows:])
            im.append(cos[rows:] - sin[:rows])
    re, im = jnp.concatenate(re, axis=1), jnp.concatenate(im, axis=1)
    power = re * re + im * im
    top, rest = split(power)
    both = dot(jnp.concatenate([top, rest], axis=0), band_ref[...])
    smooth = (both[:rows] + both[rows:]) * share
    factor = lax.rsqrt(smooth + 1e-05)
    white = jnp.concatenate([(re * factor).astype(BF16), (im * factor).astype(BF16)], axis=0)
    picked = dot(chosen, white).astype(BF16)
    width = out_ref.shape[2]
    for spot, part in enumerate(quarter_order):
        out_ref[spot] = picked[:, part * width : (part + 1) * width]
    for copy in copies[last:]:
        copy.wait()


def cross_kernel(x_ref, pick_ref, out_ref, held_ref):
    parts, _, width = x_ref.shape
    for part in range(parts):
        held_ref[:, part * width : (part + 1) * width] = dot(pick_ref[...], x_ref[part])
    for block in range(2):
        cr, ci = [0.0] * 8, [0.0] * 8
        for window in range(2):
            re = (block * 2 + window) * 48
            im = re + 24
            for part in range(parts):
                lanes = slice(part * width, (part + 1) * width)
                br = held_ref[re + 8 : re + 24, lanes]
                bi = held_ref[im + 8 : im + 24, lanes]
                for home in range(8):
                    ar = held_ref[re + home : re + home + 1, lanes]
                    ai = held_ref[im + home : im + home + 1, lanes]
                    cr[home] = cr[home] + (ar * br + ai * bi)
                    ci[home] = ci[home] + (ai * br - ar * bi)
        for home in range(8):
            r, i = cr[home], ci[home]
            terms = jnp.concatenate([r[:8], i[:8], r[8:], i[8:]], axis=0)
            terms = terms.astype(BF16)
            for side in range(2):
                row = place_order.index((block * 8 + home) * 2 + side) * 16
                out_ref[row : row + 16, :] = terms[side * 16 : side * 16 + 16]


def inverse_kernel(x_ref, table_ref, scale_ref, out_ref):
    quarter = out_ref.shape[1] // 4
    width = x_ref.shape[1]
    waves = []
    for group in range(4):
        terms = 0.0
        for source, place in enumerate(place_order):
            if place % 4 != group:
                continue
            terms = terms + x_ref[source * 16 : source * 16 + 16, :].astype(F32)
        weight = 2.0
        if group == 0:
            weight = jnp.where(iota((1, width), 1) == 0, 1.0, 2.0)
        terms = terms * weight
        cr, ci = terms[:8], terms[8:]
        side = jnp.concatenate([cr, -ci], axis=1)
        if group >= 2:
            side = jnp.concatenate([side, jnp.concatenate([ci, cr], axis=1)], axis=0)
        waves.append(product(side, table_ref[0, group], table_ref[1, group]))
    a0, a2, b1, b3 = waves
    plus, minus = a0 + a2, a0 - a2
    cos = b1[:8] + b3[:8]
    sin = b1[8:] - b3[8:]
    scale = scale_ref[0:1, 0:1]
    for i, lags in enumerate((plus - cos, minus + sin, plus + cos, minus - sin)):
        out_ref[:, i * quarter : (i + 1) * quarter] = lags * scale


VMEM = pl.BlockSpec(memory_space=pltpu.VMEM)
SMEM = pl.BlockSpec(memory_space=pltpu.SMEM)
HBM = pl.BlockSpec(memory_space=pltpu.HBM)


def call(kernel, out, operands, specs=None, scratch=()):
    return pl.pallas_call(
        kernel,
        out_shape=out,
        in_specs=specs or [VMEM] * len(operands),
        out_specs=[VMEM] * len(out) if isinstance(out, list) else VMEM,
        scratch_shapes=scratch,
        compiler_params=pltpu.CompilerParams(vmem_limit_bytes=32 * 1024 * 1024),
    )(*operands)


def body(traces, needed, home_slot, partner_slot, live_blocks):
    samples = traces.shape[2]
    bins = samples // 2
    groups = lax.axis_size("chan")
    win_count = lax.axis_size("win")
    owner = lax.axis_index("chan")
    place = lax.axis_index("win")
    per_group = 8 * needed.shape[1] // groups
    parts = 4
    width = bins // parts
    held_rows = 4 * (home_slot.size + partner_slot.size)

    table = wave_tables(samples)
    far = [
        pltpu.with_memory_space_constraint(jnp.asarray(a), pltpu.HBM)
        for a in (traces, table, table.swapaxes(2, 3), needed, home_slot, partner_slot)
    ]
    outgoing, waves, pick, scale = call(
        spectra_kernel,
        [
            jax.ShapeDtypeStruct((parts, groups * per_group, width), BF16),
            jax.ShapeDtypeStruct(table.shape, BF16),
            jax.ShapeDtypeStruct((held_rows, groups * per_group), BF16),
            jax.ShapeDtypeStruct((8, 128), F32),
        ],
        (owner[None], place[None], live_blocks, *far),
        [SMEM, SMEM, SMEM] + [HBM] * len(far),
        [
            pltpu.VMEM(traces.shape, F32),
            pltpu.VMEM(table.shape, BF16),
            pltpu.VMEM(needed.shape, I32),
            pltpu.VMEM(home_slot.shape, I32),
            pltpu.VMEM(partner_slot.shape, I32),
            pltpu.VMEM((bins, bins), BF16),
            pltpu.SemaphoreType.DMA((15,)),
        ],
    )
    near = [
        [
            o * win_count + w + q
            for q in quarter_order
            for o in owner_order
        ]
        for w in range(0, win_count, parts)
    ]
    incoming = lax.all_to_all(
        outgoing.reshape(parts * groups, per_group, width),
        ("chan", "win"),
        split_axis=0,
        concat_axis=0,
        axis_index_groups=near,
        tiled=True,
    ).reshape(parts, groups * per_group, width)
    terms = call(
        cross_kernel,
        jax.ShapeDtypeStruct((win_count * 16, width), BF16),
        (incoming, pick),
        scratch=[pltpu.VMEM((held_rows, bins), F32)],
    )
    gathered = lax.all_to_all(
        terms.reshape(win_count, 16, width),
        "win",
        split_axis=0,
        concat_axis=0,
        axis_index_groups=[list(place_order)],
        tiled=True,
    ).reshape(win_count * 16, width)
    return call(
        inverse_kernel, jax.ShapeDtypeStruct((8, samples), F32), (gathered, waves, scale)
    )


def solution(mesh):
    placed = (P("chan", "win", None), P(), P("chan", None), P("chan", None), P("chan"))
    return jax.shard_map(
        body, mesh=mesh, in_specs=placed, out_specs=P(("chan", "win"), None), check_vma=False
    )
```
